256 devices in a mesh: depth: 4 (over x), slab: 64 (over y, z, core).
Axes of the slice: x: 4, y: 4, z: 8, core: 2. Of those that a mesh axis runs over, the one named last changes fastest.
Arguments:
- incident: bfloat16 [2, 2, 1536, 1536], P(None, None, 'slab'), may hold values from -6 to 6
- transmission: bfloat16 [4, 2, 1536, 1536], P('depth', None, 'slab'), may hold values from -4.1875 to 4.1875
- prop_phase: float32 [1536, 1536], P(None, 'slab'), may hold values from -3.140625 to 3.140625
- cotangent: bfloat16 [2, 2, 1536, 1536], P(None, None, 'slab'), may hold values from -6 to 6
Outputs:
- trans_grad: float32 [4, 2, 1536, 1536], P('depth', None, 'slab')
The draws below stay inside these ranges and needn't reach their ends.
All inputs are finite; a program needn't handle non-finite values.
Results may differ from the reference program's by a relative error of at most 0.038.
Values may be sent and summed in bfloat16 or wider, within the bound.
A program may use at most 128 MiB of HBM per device.

```python
import jax
import jax.numpy as jnp
from jax import lax

N = 1536
B = 2
L = 4


def levels(rng, shape, split, least, high):
    loudness, own = 1.0, jax.random.fold_in(rng, 6)
    for position, blocks in split:
        heights = jnp.exp(jax.random.uniform(jax.random.fold_in(own, position), (blocks,), jnp.float32, least / len(split), high / len(split)))
        loudness = loudness * jnp.repeat(heights, shape[position] // blocks).reshape([-1 if axis == position else 1 for axis in range(len(shape))])
    return loudness


def bell_draw(key, dims, width, most, cuts=(), held_as=jnp.bfloat16):
    loudness = levels(key, dims, cuts, -0.22, 0.18) if cuts else 1.0
    values = jax.random.normal(key, dims, jnp.float32) * width * loudness
    return jnp.minimum(jnp.maximum(values, -most), most).astype(held_as)


def setup_inputs(seed: int = 0) -> dict:
    keys = jax.random.split(jax.random.key(seed), 5)
    return {
        "incident": bell_draw(keys[0], (B, 2, N, N), 1.0, 6.0, ((2, 64),)),
        "transmission": bell_draw(keys[1], (L, 2, N, N), 0.7, 4.1875, ((0, 4), (2, 64))),
        "prop_phase": jnp.clip(jax.random.uniform(keys[2], (N, N), jnp.float32, -3.140625, 3.140625), -3.140625, 3.140625),
        "cotangent": bell_draw(keys[3], (B, 2, N, N), 1.0, 6.0, ((2, 64),)),
    }


def rounded(value):
    real_part, imag_part = lax.optimization_barrier((jnp.real(value).astype(jnp.bfloat16), jnp.imag(value).astype(jnp.bfloat16)))
    return lax.complex(real_part.astype(jnp.float32), imag_part.astype(jnp.float32))


def as_complex(pair_array):
    return lax.complex(pair_array[:, 0].astype(jnp.float32), pair_array[:, 1].astype(jnp.float32))


def propagate(field, kernel):
    spectrum = rounded(jnp.fft.fft(field, axis=-1))
    spectrum = jnp.fft.fft(spectrum, axis=-2)
    spectrum = rounded(spectrum * kernel)
    spectrum = rounded(jnp.fft.ifft(spectrum, axis=-2))
    return rounded(jnp.fft.ifft(spectrum, axis=-1))


def reference(incident, transmission, prop_phase, cotangent):
    kern_cos = jnp.cos(prop_phase)
    kern_sin = jnp.sin(prop_phase)
    kernel = lax.complex(kern_cos, kern_sin)
    kernel_conj = lax.complex(kern_cos, -kern_sin)
    trans_all = as_complex(transmission)
    current = as_complex(incident)
    entries = []
    for slice_idx in range(L):
        entries.append(current)
        current = propagate(rounded(trans_all[slice_idx] * current), kernel)
    adjoint = as_complex(cotangent)
    grads = [None] * L
    for slice_idx in reversed(range(L)):
        pulled = propagate(adjoint, kernel_conj)
        total = jnp.sum(jnp.conj(entries[slice_idx]) * pulled, axis=0)
        grads[slice_idx] = jnp.stack([jnp.real(total), jnp.imag(total)], axis=0).astype(jnp.float32)
        adjoint = rounded(jnp.conj(trans_all[slice_idx]) * pulled)
    return jnp.stack(grads, axis=0)
```

```python
import functools
import math

import jax
import jax.numpy as jnp
import numpy as np
from jax import lax
from jax.experimental import pallas as pl
from jax.experimental.pallas import tpu as pltpu
from jax.sharding import PartitionSpec as P

N = 1536
SLABS = 64
ROWS = N // SLABS
BIG = 256
SMALL = N // BIG
KEEP = BIG // SLABS
DEPTH = 4
MESH = pl.DeviceIdType.MESH
F32 = jnp.float32
BF16 = jnp.bfloat16


def angle(x, period):
    turn = 2.0 * math.pi * (x % period) / period
    return np.cos(turn), np.sin(turn)


def block_matrix(re_re, re_im, im_re, im_im):
    return np.block([[re_re, re_im], [im_re, im_im]])


@functools.lru_cache(None)
def make_tables():
    bf = lambda a: np.asarray(a, np.float32).astype(jnp.bfloat16)
    freq = np.arange(BIG)
    samp = np.arange(BIG)
    cos, sin = angle(freq[:, None] * samp[None, :], BIG)
    full = np.zeros((SLABS, 2, KEEP, 2, BIG))
    c4, s4 = cos.reshape(SLABS, KEEP, BIG), sin.reshape(SLABS, KEEP, BIG)
    full[:, 0, :, 0], full[:, 0, :, 1] = c4, s4
    full[:, 1, :, 0], full[:, 1, :, 1] = -s4, c4
    row_fwd = full.reshape(512, 512)
    full = np.zeros((SLABS, 2, KEEP, 2, BIG))
    full[:, 0, :, 0], full[:, 0, :, 1] = c4, s4
    full[:, 1, :, 0], full[:, 1, :, 1] = -s4, c4
    row_inv = full.reshape(512, 512)
    m64 = np.arange(SLABS)
    cos, sin = angle(m64[:, None] * m64[None, :], SLABS)
    full = np.zeros((2, KEEP, SLABS, SLABS, 2, KEEP))
    back = np.zeros((SLABS, 2, KEEP, 2, KEEP, SLABS))
    for k in range(KEEP):
        full[0, k, :, :, 0, k], full[0, k, :, :, 1, k] = cos, sin
        full[1, k, :, :, 0, k], full[1, k, :, :, 1, k] = -sin, cos
        back[:, 0, k, 0, k, :], back[:, 0, k, 1, k, :] = cos, -sin
        back[:, 1, k, 0, k, :], back[:, 1, k, 1, k, :] = sin, cos
    col_fwd = full.reshape(512, 512)
    col_inv = back.reshape(512, 512)
    lane_fwd = np.zeros((2, 256, 2, 256))
    lane_inv = np.zeros((2, 256, 2, 256))
    rho = np.arange(ROWS)
    cos, sin = angle(rho[:, None] * rho[None, :], ROWS)
    for j in range(SMALL):
        a = 24 * j + rho[:, None]
        b = 8 * rho[None, :] + j
        lane_fwd[0, a, 0, b], lane_fwd[1, a, 0, b] = cos, sin
        lane_fwd[0, a, 1, b], lane_fwd[1, a, 1, b] = -sin, cos
        lane_inv[0, b, 0, a], lane_inv[1, b, 0, a] = cos, -sin
        lane_inv[0, b, 1, a], lane_inv[1, b, 1, a] = sin, cos
    lane_fwd = lane_fwd.reshape(512, 512)
    lane_inv = lane_inv.reshape(512, 512)
    cos, sin = angle(np.arange(SMALL)[:, None] * samp[None, :], N)
    row_tw = np.zeros((2, 8, BIG))
    row_tw[0, :SMALL], row_tw[1, :SMALL] = cos, sin
    cos, sin = angle(m64[:, None] * rho[None, :], N)
    col_tw = np.zeros((2, SLABS, 256))
    for j in range(SMALL):
        col_tw[0, :, 24 * j : 24 * j + 24] = cos
        col_tw[1, :, 24 * j : 24 * j + 24] = sin
    mats = np.stack([row_fwd, col_fwd, lane_fwd, lane_inv, col_inv, row_inv])
    return bf(mats), row_tw.astype(np.float32), col_tw.astype(np.float32)


def dot(a, b, dims=((1,), (0,))):
    return lax.dot_general(a, b, (dims, ((), ())), preferred_element_type=F32)


def dft_three(x, orient):
    (ar, ai), (br, bi), (cr, ci) = x
    tr, ti = br + cr, bi + ci
    er, ei = (br - cr) * (orient * math.sqrt(0.75)), (bi - ci) * (orient * math.sqrt(0.75))
    mr, mi = ar - 0.5 * tr, ai - 0.5 * ti
    return (ar + tr, ai + ti), (mr + ei, mi - er), (mr - ei, mi + er)


def dft_six(x, orient):
    out = [None] * 6
    for k1 in range(2):
        sums = []
        for n2 in range(3):
            (ar, ai), (br, bi) = x[(2 * n2) % 6], x[(3 + 2 * n2) % 6]
            sums.append((ar + br, ai + bi) if k1 == 0 else (ar - br, ai - bi))
        three = dft_three(sums, orient)
        for k2 in range(3):
            out[(3 * k1 + 4 * k2) % 6] = three[k2]
    return out


def pack(y):
    both = [y[:, :128].reshape(SLABS, 8, 128), y[:, 128:].reshape(SLABS, 8, 128)]
    return jnp.concatenate(both, axis=1).astype(BF16)


def unpack(x):
    x = x.astype(F32)
    both = [x[:, :8].reshape(512, 128), x[:, 8:].reshape(512, 128)]
    return jnp.concatenate(both, axis=1).astype(BF16)


def hop(a, n):
    return min(a, n - a)


def slab_order():
    offs = [(y, z, c) for y in range(4) for z in range(8) for c in range(2)][1:]
    offs.sort(key=lambda t: (-(hop(t[0], 4) + hop(t[1], 8)), t[2], t[1], t[0]))
    plus = [t for t in offs if 0 < t[1] < 4]
    minus = [t for t in offs if t[1] > 4]
    rest = [t for t in offs if t[1] in (0, 4)]
    out = []
    for i in range(len(plus)):
        out += [plus[i], minus[i]] + rest[i : i + 1]
    return out + rest[len(plus) :]


def kernel(inc, trans, phase, cot, mats, row_tw, col_tw, out,
           tbuf, cur, zbuf, send1, recv1, send2, recv2, results, hbuf, pbuf, outgoing,
           a2a_send, a2a_recv, t_send, t_recv, r_send, r_recv):
    depth = lax.axis_index("depth")
    slab = lax.axis_index("slab")
    y0, z0, c0 = slab // 16, (slab // 2) % 8, slab % 2
    forward = depth >= 2
    adjoint = depth < 2
    partners = [
        lax.rem(y0 + dy, 4) * 16 + lax.rem(z0 + dz, 8) * 2 + lax.rem(c0 + dc, 2)
        for dy, dz, dc in slab_order()
    ]
    others = [lax.rem(depth + o, DEPTH) for o in range(1, DEPTH)]

    barrier = pltpu.get_barrier_semaphore()
    for p in partners:
        pl.semaphore_signal(barrier, inc=1, device_id=(depth, p), device_id_type=MESH)
    for d in others:
        pl.semaphore_signal(barrier, inc=1, device_id=(d, slab), device_id_type=MESH)

    tbuf[depth] = trans[...]
    zbuf[144:, :] = jnp.zeros((112, 512), F32)

    @pl.when(adjoint)
    def _():
        cur[...] = cot[lax.rem(depth, 2)].astype(F32)

    @pl.when(depth == 0)
    def _():
        results[2] = inc[0]
        results[3] = inc[1]

    pl.semaphore_wait(barrier, len(partners) + len(others))

    def t_copy(d):
        return pltpu.make_async_remote_copy(
            src_ref=trans, dst_ref=tbuf.at[depth], send_sem=t_send.at[d], recv_sem=t_recv.at[depth],
            device_id=(d, slab), device_id_type=MESH)

    def t_needed(source, target):
        return jnp.where(target < 2, source >= 1, source <= 2)

    for d in others:
        @pl.when(t_needed(depth, d))
        def _(d=d):
            t_copy(d).start()

    def t_arrived(which):
        @pl.when(which != depth)
        def _():
            pltpu.make_async_copy(trans, tbuf.at[which], t_recv.at[which]).wait()

    orient = jnp.where(forward, 1.0, -1.0).astype(F32)

    def multiply(field, which):
        f = field.astype(F32)
        t = tbuf[which].astype(F32)
        fr, fi, tr, ti = f[:ROWS], f[ROWS:], t[:ROWS], t[ROWS:] * orient
        cur[:ROWS] = (fr * tr - fi * ti).astype(BF16).astype(F32)
        cur[ROWS:] = (fr * ti + fi * tr).astype(BF16).astype(F32)

    @pl.when(forward)
    def _():
        t_arrived(0)
        multiply(inc[lax.rem(depth, 2)], 0)

    def exchange(which, sent, received):
        for p in partners:
            pltpu.make_async_remote_copy(
                src_ref=sent.at[p], dst_ref=received.at[slab], send_sem=a2a_send.at[which],
                recv_sem=a2a_recv.at[which], device_id=(depth, p), device_id_type=MESH).start()
        received[slab] = sent[slab]

    def finish(which, sent, received):
        part = received.at[pl.ds(0, SLABS - 1)]
        pltpu.make_async_copy(part, part, a2a_recv.at[which]).wait()
        part = sent.at[pl.ds(0, SLABS - 1)]
        pltpu.make_async_copy(part, part, a2a_send.at[which]).wait()

    def stage_a():
        for half in range(2):
            lo = 128 * half
            x = [(cur[:ROWS, BIG * a + lo : BIG * a + lo + 128], cur[ROWS:, BIG * a + lo : BIG * a + lo + 128])
                 for a in range(SMALL)]
            for j, (zr, zi) in enumerate(dft_six(x, 1.0)):
                c = row_tw[0, j : j + 1, lo : lo + 128]
                s = row_tw[1, j : j + 1, lo : lo + 128]
                zbuf[ROWS * j : ROWS * j + ROWS, lo : lo + 128] = zr * c + zi * s
                zbuf[ROWS * j : ROWS * j + ROWS, BIG + lo : BIG + lo + 128] = zi * c - zr * s
        send1[...] = pack(dot(mats[0], zbuf[...].astype(BF16), ((1,), (1,))))

    def make_filter():
        lane = lax.broadcasted_iota(jnp.int32, (SLABS, 128), 1)
        for k in range(KEEP):
            for chunk in range(2):
                hbuf[0, 64 * k : 64 * k + 64, 128 * chunk : 128 * chunk + 128] = jnp.zeros((64, 128), F32)
        pbuf[...] = jnp.zeros_like(pbuf)
        for chunk, count in ((0, 16), (1, 8)):
            acc = [jnp.zeros((SLABS, 128), F32) for _ in range(KEEP)]
            for i in range(count):
                p = 16 * chunk + i
                pbuf[:, :ROWS] = phase[64 * p : 64 * p + 64, :]
                block = pbuf[...]
                inside = (lane >= 8 * i) & (lane < 8 * i + SMALL)
                for k in range(KEEP):
                    moved = pltpu.roll(block, (8 * i - SMALL * k) % 128, 1)
                    acc[k] = jnp.where(inside, moved, acc[k])
            for k in range(KEEP):
                hbuf[0, 64 * k : 64 * k + 64, 128 * chunk : 128 * chunk + 128] = jnp.cos(acc[k])
                hbuf[1, 64 * k : 64 * k + 64, 128 * chunk : 128 * chunk + 128] = jnp.sin(acc[k]) * orient

    def stage_b():
        y = dot(mats[1], unpack(recv1[...]))
        c, s = col_tw[0][None], col_tw[1][None]
        yr, yi = y[:256].reshape(KEEP, 64, 256), y[256:].reshape(KEEP, 64, 256)
        z = jnp.concatenate([(yr * c + yi * s).reshape(256, 256), (yi * c - yr * s).reshape(256, 256)], axis=1)
        y = dot(z.astype(BF16), mats[2])
        yr, yi, hr, hi = y[:, :256], y[:, 256:], hbuf[0], hbuf[1]
        z = jnp.concatenate([yr * hr - yi * hi, yi * hr + yr * hi], axis=1)
        y = dot(z.astype(BF16), mats[3])
        yr, yi = y[:, :256].reshape(KEEP, 64, 256), y[:, 256:].reshape(KEEP, 64, 256)
        c, s = c * (1.0 / N), s * (1.0 / N)
        z = jnp.concatenate([(yr * c - yi * s).reshape(256, 256), (yi * c + yr * s).reshape(256, 256)], axis=0)
        send2[...] = pack(dot(mats[4], z.astype(BF16)))

    def stage_c(turn):
        zbuf_c = dot(unpack(recv2[...]), mats[5], ((0,), (0,)))
        for half in range(2):
            lo = 128 * half
            x = []
            for j in range(SMALL):
                c = row_tw[0, j : j + 1, lo : lo + 128] * (1.0 / N)
                s = row_tw[1, j : j + 1, lo : lo + 128] * (1.0 / N)
                zr = zbuf_c[ROWS * j : ROWS * j + ROWS, lo : lo + 128]
                zi = zbuf_c[ROWS * j : ROWS * j + ROWS, BIG + lo : BIG + lo + 128]
                x.append((zr * c - zi * s, zi * c + zr * s))
            for a, (vr, vi) in enumerate(dft_six(x, -1.0)):
                both = jnp.concatenate([vr, vi], axis=0)
                outgoing[turn, :, BIG * a + lo : BIG * a + lo + 128] = both.astype(BF16)

    def r_copy(turn, target):
        return pltpu.make_async_remote_copy(
            src_ref=outgoing.at[turn], dst_ref=results.at[depth], send_sem=r_send.at[turn],
            recv_sem=r_recv.at[depth], device_id=(target, slab), device_id_type=MESH)

    def target_of(turn):
        return jnp.where(forward, turn + 1, DEPTH - 1 - turn)

    @pl.loop(0, DEPTH)
    def _(turn):
        @pl.when(adjoint | (turn < DEPTH - 1))
        def _():
            stage_a()
            exchange(0, send1, recv1)

            @pl.when(turn == 0)
            def _():
                make_filter()

            finish(0, send1, recv1)
            stage_b()
            exchange(1, send2, recv2)
            finish(1, send2, recv2)
            stage_c(turn)
            target = target_of(turn)

            @pl.when(target != depth)
            def _():
                r_copy(turn, target).start()

            @pl.when(target == depth)
            def _():
                results[depth] = outgoing[turn]

            @pl.when(jnp.where(forward, turn < DEPTH - 2, turn < DEPTH - 1))
            def _():
                t_arrived(target)
                multiply(outgoing[turn], target)

    for slot in range(DEPTH):
        @pl.when((depth != slot) & ((slot < 2) | (depth >= 1)))
        def _(slot=slot):
            pltpu.make_async_copy(trans, results.at[slot], r_recv.at[slot]).wait()

    gr = jnp.zeros((ROWS, N), F32)
    gi = jnp.zeros((ROWS, N), F32)
    for m in range(2):
        u = results[2 + m].astype(F32)
        p = results[m].astype(F32)
        ur, ui, pr, pi = u[:ROWS], u[ROWS:], p[:ROWS], p[ROWS:]
        gr = gr + (ur * pr + ui * pi)
        gi = gi + (ur * pi - ui * pr)
    out[:ROWS] = gr
    out[ROWS:] = gi

    for d in others:
        @pl.when(t_needed(depth, d))
        def _(d=d):
            t_copy(d).wait_send()

    for turn in range(DEPTH):
        target = target_of(turn)

        @pl.when((target != depth) & (adjoint | (turn < DEPTH - 1)))
        def _(turn=turn, target=target):
            r_copy(turn, target).wait_send()


def on_device(incident, transmission, prop_phase, cotangent):
    mats, row_tw, col_tw = (jnp.asarray(t) for t in make_tables())
    inc = incident.reshape(2, 2 * ROWS, N)
    trans = transmission.reshape(2 * ROWS, N)
    cot = cotangent.reshape(2, 2 * ROWS, N)
    vmem = pl.BlockSpec(memory_space=pltpu.VMEM)
    field = (2 * ROWS, N)
    message = (SLABS, 16, 128)
    dma = pltpu.SemaphoreType.DMA
    grads = pl.pallas_call(
        kernel,
        out_shape=jax.ShapeDtypeStruct(field, F32),
        in_specs=[vmem] * 7,
        out_specs=vmem,
        scratch_shapes=[
            pltpu.VMEM((DEPTH,) + field, BF16),
            pltpu.VMEM(field, F32),
            pltpu.VMEM((256, 512), F32),
            pltpu.VMEM(message, BF16),
            pltpu.VMEM(message, BF16),
            pltpu.VMEM(message, BF16),
            pltpu.VMEM(message, BF16),
            pltpu.VMEM((DEPTH,) + field, BF16),
            pltpu.VMEM((2, 256, 256), F32),
            pltpu.VMEM((SLABS, 128), F32),
            pltpu.VMEM((DEPTH,) + field, BF16),
            dma((2,)), dma((2,)), dma((DEPTH,)), dma((DEPTH,)), dma((DEPTH,)), dma((DEPTH,)),
        ],
        compiler_params=pltpu.CompilerParams(
            collective_id=0, has_side_effects=True, vmem_limit_bytes=48 * 2**20),
        name="chains",
    )(inc, trans, prop_phase, cot, mats, row_tw, col_tw)
    return grads.reshape(1, 2, ROWS, N)


def solution(mesh):
    in_specs = (
        P(None, None, "slab", None),
        P("depth", None, "slab", None),
        P(None, "slab"),
        P(None, None, "slab", None),
    )
    out_specs = P("depth", None, "slab", None)
    return jax.shard_map(
        on_device, mesh=mesh, in_specs=in_specs, out_specs=out_specs, check_vma=False
    )
```

```python
import functools
import math

import jax
import jax.numpy as jnp
import numpy as np
from jax import lax
from jax.experimental import pallas as pl
from jax.experimental.pallas import tpu as pltpu
from jax.sharding import PartitionSpec as P

N = 1536
SLABS = 64
ROWS = N // SLABS
BIG = 256
SMALL = N // BIG
KEEP = BIG // SLABS
DEPTH = 4
MESH = pl.DeviceIdType.MESH
F32 = jnp.float32
BF16 = jnp.bfloat16


def angle(x, period):
    turn = 2.0 * math.pi * (x % period) / period
    return np.cos(turn), np.sin(turn)


def block_matrix(re_re, re_im, im_re, im_im):
    return np.block([[re_re, re_im], [im_re, im_im]])


@functools.lru_cache(None)
def make_tables():
    bf = lambda a: np.asarray(a, np.float32).astype(jnp.bfloat16)
    freq = np.arange(BIG)
    samp = np.arange(BIG)
    cos, sin = angle(freq[:, None] * samp[None, :], BIG)
    full = np.zeros((SLABS, 2, KEEP, 2, BIG))
    c4, s4 = cos.reshape(SLABS, KEEP, BIG), sin.reshape(SLABS, KEEP, BIG)
    full[:, 0, :, 0], full[:, 0, :, 1] = c4, s4
    full[:, 1, :, 0], full[:, 1, :, 1] = -s4, c4
    row_fwd = full.reshape(512, 512)
    full = np.zeros((SLABS, 2, KEEP, 2, BIG))
    full[:, 0, :, 0], full[:, 0, :, 1] = c4, s4
    full[:, 1, :, 0], full[:, 1, :, 1] = -s4, c4
    row_inv = full.reshape(512, 512)
    m64 = np.arange(SLABS)
    cos, sin = angle(m64[:, None] * m64[None, :], SLABS)
    full = np.zeros((2, KEEP, SLABS, SLABS, 2, KEEP))
    back = np.zeros((SLABS, 2, KEEP, 2, KEEP, SLABS))
    for k in range(KEEP):
        full[0, k, :, :, 0, k], full[0, k, :, :, 1, k] = cos, sin
        full[1, k, :, :, 0, k], full[1, k, :, :, 1, k] = -sin, cos
        back[:, 0, k, 0, k, :], back[:, 0, k, 1, k, :] = cos, -sin
        back[:, 1, k, 0, k, :], back[:, 1, k, 1, k, :] = sin, cos
    col_fwd = full.reshape(512, 512)
    col_inv = back.reshape(512, 512)
    lane_fwd = np.zeros((2, 256, 2, 256))
    lane_inv = np.zeros((2, 256, 2, 256))
    rho = np.arange(ROWS)
    cos, sin = angle(rho[:, None] * rho[None, :], ROWS)
    for j in range(SMALL):
        a = 24 * j + rho[:, None]
        b = 8 * rho[None, :] + j
        lane_fwd[0, a, 0, b], lane_fwd[1, a, 0, b] = cos, sin
        lane_fwd[0, a, 1, b], lane_fwd[1, a, 1, b] = -sin, cos
        lane_inv[0, b, 0, a], lane_inv[1, b, 0, a] = cos, -sin
        lane_inv[0, b, 1, a], lane_inv[1, b, 1, a] = sin, cos
    lane_fwd = lane_fwd.reshape(512, 512)
    lane_inv = lane_inv.reshape(512, 512)
    cos, sin = angle(np.arange(SMALL)[:, None] * samp[None, :], N)
    row_tw = np.zeros((2, 8, BIG))
    row_tw[0, :SMALL], row_tw[1, :SMALL] = cos, sin
    cos, sin = angle(m64[:, None] * rho[None, :], N)
    col_tw = np.zeros((2, SLABS, 256))
    for j in range(SMALL):
        col_tw[0, :, 24 * j : 24 * j + 24] = cos
        col_tw[1, :, 24 * j : 24 * j + 24] = sin
    mats = np.stack([row_fwd, col_fwd, lane_fwd, lane_inv, col_inv, row_inv])
    return bf(mats), row_tw.astype(np.float32), col_tw.astype(np.float32)


def dot(a, b, dims=((1,), (0,))):
    return lax.dot_general(a, b, (dims, ((), ())), preferred_element_type=F32)


def dft_three(x, orient):
    (ar, ai), (br, bi), (cr, ci) = x
    tr, ti = br + cr, bi + ci
    er, ei = (br - cr) * (orient * math.sqrt(0.75)), (bi - ci) * (orient * math.sqrt(0.75))
    mr, mi = ar - 0.5 * tr, ai - 0.5 * ti
    return (ar + tr, ai + ti), (mr + ei, mi - er), (mr - ei, mi + er)


def dft_six(x, orient):
    out = [None] * 6
    for k1 in range(2):
        sums = []
        for n2 in range(3):
            (ar, ai), (br, bi) = x[(2 * n2) % 6], x[(3 + 2 * n2) % 6]
            sums.append((ar + br, ai + bi) if k1 == 0 else (ar - br, ai - bi))
        three = dft_three(sums, orient)
        for k2 in range(3):
            out[(3 * k1 + 4 * k2) % 6] = three[k2]
    return out


def pack(y, main, rest, fold):
    main[...] = y[:, :128].reshape(SLABS, 8, 128).astype(BF16)
    fold[...] = y[:, 128:]
    row = fold[pl.ds(0, SLABS, stride=8), :]
    for i in range(1, 8):
        row = row + pltpu.roll(fold[pl.ds(i, SLABS, stride=8), :], 16 * i, 1)
    rest[...] = row.reshape(SLABS, 1, 128)


def unpack(main, rest, fold):
    row = rest[...].reshape(SLABS, 128)
    fold[pl.ds(0, SLABS, stride=8), :] = row
    for i in range(1, 8):
        fold[pl.ds(i, SLABS, stride=8), :] = pltpu.roll(row, 128 - 16 * i, 1)
    both = [main[...].astype(F32).reshape(512, 128), fold[...]]
    return jnp.concatenate(both, axis=1).astype(BF16)


def hop(a, n):
    return min(a, n - a)


def slab_order():
    offs = [(y, z, c) for y in range(4) for z in range(8) for c in range(2)][1:]
    offs.sort(key=lambda t: (-(hop(t[0], 4) + hop(t[1], 8)), t[2], t[1], t[0]))
    plus = [t for t in offs if 0 < t[1] < 4]
    minus = [t for t in offs if t[1] > 4]
    rest = [t for t in offs if t[1] in (0, 4)]
    out = []
    for i in range(len(plus)):
        out += [plus[i], minus[i]] + rest[i : i + 1]
    return out + rest[len(plus) :]


def kernel(inc_hbm, trans_hbm, phase_hbm, cot_hbm, mats_hbm, row_tw_hbm, col_tw_hbm, out,
           field, phase, mats, row_tw, col_tw,
           tbuf, cur, zbuf, fold, send1, send1r, recv1, recv1r, send2, send2r, recv2, recv2r,
           results, hbuf, pbuf, outgoing,
           load, load_mat, a2a_send, a2a_recv, t_send, t_recv, r_send, r_recv):
    depth = lax.axis_index("depth")
    slab = lax.axis_index("slab")
    y0, z0, c0 = slab // 16, (slab // 2) % 8, slab % 2
    forward = depth >= 2
    adjoint = depth < 2
    which_field = lax.rem(depth, 2)
    partners = [
        lax.rem(y0 + dy, 4) * 16 + lax.rem(z0 + dz, 8) * 2 + lax.rem(c0 + dc, 2)
        for dy, dz, dc in slab_order()
    ]
    others = [lax.rem(depth + o, DEPTH) for o in range(1, DEPTH)]

    @pl.when(adjoint)
    def _():
        pltpu.make_async_copy(cot_hbm.at[which_field], field, load.at[0]).start()

    @pl.when(forward)
    def _():
        pltpu.make_async_copy(inc_hbm.at[which_field], field, load.at[0]).start()

    loads = [
        pltpu.make_async_copy(row_tw_hbm, row_tw, load.at[1]),
        pltpu.make_async_copy(col_tw_hbm, col_tw, load.at[2]),
        pltpu.make_async_copy(phase_hbm, phase, load.at[3]),
        pltpu.make_async_copy(trans_hbm, tbuf.at[depth], load.at[4]),
    ]
    mat_loads = [pltpu.make_async_copy(mats_hbm.at[k], mats.at[k], load_mat.at[k]) for k in range(6)]
    loads[0].start()
    mat_loads[0].start()
    for copy in loads[1:] + mat_loads[1:]:
        copy.start()

    @pl.when(depth == 0)
    def _():
        for m in range(2):
            pltpu.make_async_copy(inc_hbm.at[m], results.at[2 + m], load.at[5 + m]).start()

    barrier = pltpu.get_barrier_semaphore()
    for p in partners:
        pl.semaphore_signal(barrier, inc=1, device_id=(depth, p), device_id_type=MESH)
    for d in others:
        pl.semaphore_signal(barrier, inc=1, device_id=(d, slab), device_id_type=MESH)

    zbuf[144:, :] = jnp.zeros((112, 512), F32)
    orient = jnp.where(forward, 1.0, -1.0).astype(F32)

    def t_copy(d):
        return pltpu.make_async_remote_copy(
            src_ref=trans_hbm, dst_ref=tbuf.at[depth], send_sem=t_send.at[d], recv_sem=t_recv.at[depth],
            device_id=(d, slab), device_id_type=MESH)

    def t_needed(source, target):
        return jnp.where(target < 2, source >= 1, source <= 2)

    def t_arrived(which):
        @pl.when(which != depth)
        def _():
            pltpu.make_async_copy(field, tbuf.at[which], t_recv.at[which]).wait()

    def multiply(values, which):
        f = values.astype(F32)
        t = tbuf[which].astype(F32)
        fr, fi, tr, ti = f[:ROWS], f[ROWS:], t[:ROWS], t[ROWS:] * orient
        cur[:ROWS] = (fr * tr - fi * ti).astype(BF16).astype(F32)
        cur[ROWS:] = (fr * ti + fi * tr).astype(BF16).astype(F32)

    def exchange(which, sent, sent_rest, received, received_rest):
        for p in partners:
            pltpu.make_async_remote_copy(
                src_ref=sent.at[p], dst_ref=received.at[slab], send_sem=a2a_send.at[which, 0],
                recv_sem=a2a_recv.at[which, 0], device_id=(depth, p), device_id_type=MESH).start()
            pltpu.make_async_remote_copy(
                src_ref=sent_rest.at[p], dst_ref=received_rest.at[slab], send_sem=a2a_send.at[which, 1],
                recv_sem=a2a_recv.at[which, 1], device_id=(depth, p), device_id_type=MESH).start()
        received[slab] = sent[slab]
        received_rest[slab] = sent_rest[slab]

    def finish(which, sent, sent_rest, received, received_rest):
        for k, ref, sem in ((0, sent, a2a_send), (1, sent_rest, a2a_send),
                            (0, received, a2a_recv), (1, received_rest, a2a_recv)):
            part = ref.at[pl.ds(0, SLABS - 1)]
            pltpu.make_async_copy(part, part, sem.at[which, k]).wait()

    def stage_a():
        for half in range(2):
            lo = 128 * half
            x = [(cur[:ROWS, BIG * a + lo : BIG * a + lo + 128], cur[ROWS:, BIG * a + lo : BIG * a + lo + 128])
                 for a in range(SMALL)]
            for j, (zr, zi) in enumerate(dft_six(x, 1.0)):
                c = row_tw[0, j : j + 1, lo : lo + 128]
                s = row_tw[1, j : j + 1, lo : lo + 128]
                zbuf[ROWS * j : ROWS * j + ROWS, lo : lo + 128] = zr * c + zi * s
                zbuf[ROWS * j : ROWS * j + ROWS, BIG + lo : BIG + lo + 128] = zi * c - zr * s
        pack(dot(mats[0], zbuf[...].astype(BF16), ((1,), (1,))), send1, send1r, fold)

    def make_filter():
        lane = lax.broadcasted_iota(jnp.int32, (SLABS, 128), 1)
        pbuf[...] = jnp.zeros_like(pbuf)
        for chunk, count in ((0, 16), (1, 8)):
            acc = [jnp.zeros((SLABS, 128), F32) for _ in range(KEEP)]
            for i in range(count):
                if i % 2 == 0:
                    lo = 64 * (16 * chunk + i)
                    pbuf[:ROWS] = phase[:, lo : lo + 128]
                    turned = pbuf[...].T
                block = turned[64 * (i % 2) : 64 * (i % 2) + 64]
                inside = (lane >= 8 * i) & (lane < 8 * i + SMALL)
                for k in range(KEEP):
                    moved = pltpu.roll(block, (8 * i - SMALL * k) % 128, 1)
                    acc[k] = jnp.where(inside, moved, acc[k])
            for k in range(KEEP):
                hbuf[0, 64 * k : 64 * k + 64, 128 * chunk : 128 * chunk + 128] = jnp.cos(acc[k])
                hbuf[1, 64 * k : 64 * k + 64, 128 * chunk : 128 * chunk + 128] = jnp.sin(acc[k]) * orient

    def stage_b():
        y = dot(mats[1], unpack(recv1, recv1r, fold))
        c, s = col_tw[0][None], col_tw[1][None]
        yr, yi = y[:256].reshape(KEEP, 64, 256), y[256:].reshape(KEEP, 64, 256)
        z = jnp.concatenate([(yr * c + yi * s).reshape(256, 256), (yi * c - yr * s).reshape(256, 256)], axis=1)
        y = dot(z.astype(BF16), mats[2])
        yr, yi, hr, hi = y[:, :256], y[:, 256:], hbuf[0], hbuf[1]
        z = jnp.concatenate([yr * hr - yi * hi, yi * hr + yr * hi], axis=1)
        y = dot(z.astype(BF16), mats[3])
        yr, yi = y[:, :256].reshape(KEEP, 64, 256), y[:, 256:].reshape(KEEP, 64, 256)
        c, s = c * (1.0 / N), s * (1.0 / N)
        z = jnp.concatenate([(yr * c - yi * s).reshape(256, 256), (yi * c + yr * s).reshape(256, 256)], axis=0)
        pack(dot(mats[4], z.astype(BF16)), send2, send2r, fold)

    def stage_c(turn):
        zbuf_c = dot(unpack(recv2, recv2r, fold), mats[5], ((0,), (0,)))
        for half in range(2):
            lo = 128 * half
            x = []
            for j in range(SMALL):
                c = row_tw[0, j : j + 1, lo : lo + 128] * (1.0 / N)
                s = row_tw[1, j : j + 1, lo : lo + 128] * (1.0 / N)
                zr = zbuf_c[ROWS * j : ROWS * j + ROWS, lo : lo + 128]
                zi = zbuf_c[ROWS * j : ROWS * j + ROWS, BIG + lo : BIG + lo + 128]
                x.append((zr * c - zi * s, zi * c + zr * s))
            for a, (vr, vi) in enumerate(dft_six(x, -1.0)):
                both = jnp.concatenate([vr, vi], axis=0)
                outgoing[turn, :, BIG * a + lo : BIG * a + lo + 128] = both.astype(BF16)

    def r_copy(turn, target):
        return pltpu.make_async_remote_copy(
            src_ref=outgoing.at[turn], dst_ref=results.at[depth], send_sem=r_send.at[turn],
            recv_sem=r_recv.at[depth], device_id=(target, slab), device_id_type=MESH)

    def target_of(turn):
        return jnp.where(forward, turn + 1, DEPTH - 1 - turn)

    pltpu.make_async_copy(inc_hbm.at[0], field, load.at[0]).wait()
    loads[0].wait()
    mat_loads[0].wait()

    @pl.when(adjoint)
    def _():
        cur[...] = field[...].astype(F32)
        stage_a()

    loads[3].wait()
    loads[2].wait()
    make_filter()
    pl.semaphore_wait(barrier, len(partners) + len(others))

    for d in others:
        @pl.when(t_needed(depth, d))
        def _(d=d):
            t_copy(d).start()

    @pl.when(forward)
    def _():
        t_arrived(0)
        multiply(field[...], 0)
        stage_a()

    for copy in loads[1:2] + mat_loads[1:]:
        copy.wait()

    @pl.loop(0, DEPTH)
    def _(turn):
        @pl.when(adjoint | (turn < DEPTH - 1))
        def _():
            first = send1, send1r, recv1, recv1r
            second = send2, send2r, recv2, recv2r
            exchange(0, *first)
            finish(0, *first)
            stage_b()
            exchange(1, *second)
            finish(1, *second)
            stage_c(turn)
            target = target_of(turn)

            @pl.when(target != depth)
            def _():
                r_copy(turn, target).start()

            @pl.when(target == depth)
            def _():
                results[depth] = outgoing[turn]

            @pl.when(jnp.where(forward, turn < DEPTH - 2, turn < DEPTH - 1))
            def _():
                t_arrived(target)
                multiply(outgoing[turn], target)
                stage_a()

    @pl.when(depth == 0)
    def _():
        for m in range(2):
            pltpu.make_async_copy(inc_hbm.at[m], results.at[2 + m], load.at[5 + m]).wait()

    for slot in range(DEPTH):
        @pl.when((depth != slot) & ((slot < 2) | (depth >= 1)))
        def _(slot=slot):
            pltpu.make_async_copy(field, results.at[slot], r_recv.at[slot]).wait()

    gr = jnp.zeros((ROWS, N), F32)
    gi = jnp.zeros((ROWS, N), F32)
    for m in range(2):
        u = results[2 + m].astype(F32)
        p = results[m].astype(F32)
        ur, ui, pr, pi = u[:ROWS], u[ROWS:], p[:ROWS], p[ROWS:]
        gr = gr + (ur * pr + ui * pi)
        gi = gi + (ur * pi - ui * pr)
    out[:ROWS] = gr
    out[ROWS:] = gi

    for d in others:
        @pl.when(t_needed(depth, d))
        def _(d=d):
            t_copy(d).wait_send()

    for turn in range(DEPTH):
        target = target_of(turn)

        @pl.when((target != depth) & (adjoint | (turn < DEPTH - 1)))
        def _(turn=turn, target=target):
            r_copy(turn, target).wait_send()


def on_device(incident, transmission, prop_phase, cotangent):
    mats, row_tw, col_tw = (jnp.asarray(t) for t in make_tables())
    inc = incident.reshape(2, 2 * ROWS, N)
    trans = transmission.reshape(2 * ROWS, N)
    cot = cotangent.reshape(2, 2 * ROWS, N)
    hbm = pl.BlockSpec(memory_space=pltpu.HBM)
    field = (2 * ROWS, N)
    main = pltpu.VMEM((SLABS, 8, 128), BF16)
    rest = pltpu.VMEM((SLABS, 1, 128), F32)
    dma = pltpu.SemaphoreType.DMA
    grads = pl.pallas_call(
        kernel,
        out_shape=jax.ShapeDtypeStruct(field, F32),
        in_specs=[hbm] * 7,
        out_specs=pl.BlockSpec(memory_space=pltpu.VMEM),
        scratch_shapes=[
            pltpu.VMEM(field, BF16),
            pltpu.VMEM((ROWS, N), F32),
            pltpu.VMEM(mats.shape, BF16),
            pltpu.VMEM(row_tw.shape, F32),
            pltpu.VMEM(col_tw.shape, F32),
            pltpu.VMEM((DEPTH,) + field, BF16),
            pltpu.VMEM(field, F32),
            pltpu.VMEM((256, 512), F32),
            pltpu.VMEM((512, 128), F32),
            main, rest, main, rest, main, rest, main, rest,
            pltpu.VMEM((DEPTH,) + field, BF16),
            pltpu.VMEM((2, 256, 256), F32),
            pltpu.VMEM((128, 128), F32),
            pltpu.VMEM((DEPTH,) + field, BF16),
            dma((7,)), dma((6,)), dma((2, 2)), dma((2, 2)),
            dma((DEPTH,)), dma((DEPTH,)), dma((DEPTH,)), dma((DEPTH,)),
        ],
        compiler_params=pltpu.CompilerParams(
            collective_id=0, has_side_effects=True, vmem_limit_bytes=62 * 2**20),
        name="chains",
    )(inc, trans, prop_phase.T, cot, mats, row_tw, col_tw)
    return grads.reshape(1, 2, ROWS, N)


def solution(mesh):
    in_specs = (
        P(None, None, "slab", None),
        P("depth", None, "slab", None),
        P(None, "slab"),
        P(None, None, "slab", None),
    )
    out_specs = P("depth", None, "slab", None)
    return jax.shard_map(
        on_device, mesh=mesh, in_specs=in_specs, out_specs=out_specs, check_vma=False
    )
```

```python
import functools
import math

import jax
import jax.numpy as jnp
import numpy as np
from jax import lax
from jax.experimental import pallas as pl
from jax.experimental.pallas import tpu as pltpu
from jax.sharding import PartitionSpec as P

N = 1536
SLABS = 64
ROWS = N // SLABS
BIG = 256
SMALL = N // BIG
KEEP = BIG // SLABS
DEPTH = 4
MESH = pl.DeviceIdType.MESH
F32 = jnp.float32
BF16 = jnp.bfloat16


def angle(x, period):
    turn = 2.0 * math.pi * (x % period) / period
    return np.cos(turn), np.sin(turn)


def block_matrix(re_re, re_im, im_re, im_im):
    return np.block([[re_re, re_im], [im_re, im_im]])


@functools.lru_cache(None)
def make_tables():
    bf = lambda a: np.asarray(a, np.float32).astype(jnp.bfloat16)
    freq = np.arange(BIG)
    samp = np.arange(BIG)
    cos, sin = angle(freq[:, None] * samp[None, :], BIG)
    full = np.zeros((SLABS, 2, KEEP, 2, BIG))
    c4, s4 = cos.reshape(SLABS, KEEP, BIG), sin.reshape(SLABS, KEEP, BIG)
    full[:, 0, :, 0], full[:, 0, :, 1] = c4, s4
    full[:, 1, :, 0], full[:, 1, :, 1] = -s4, c4
    row_fwd = full.reshape(512, 512)
    full = np.zeros((SLABS, 2, KEEP, 2, BIG))
    full[:, 0, :, 0], full[:, 0, :, 1] = c4, s4
    full[:, 1, :, 0], full[:, 1, :, 1] = -s4, c4
    row_inv = full.reshape(512, 512)
    m64 = np.arange(SLABS)
    cos, sin = angle(m64[:, None] * m64[None, :], SLABS)
    full = np.zeros((2, KEEP, SLABS, SLABS, 2, KEEP))
    back = np.zeros((SLABS, 2, KEEP, 2, KEEP, SLABS))
    for k in range(KEEP):
        full[0, k, :, :, 0, k], full[0, k, :, :, 1, k] = cos, sin
        full[1, k, :, :, 0, k], full[1, k, :, :, 1, k] = -sin, cos
        back[:, 0, k, 0, k, :], back[:, 0, k, 1, k, :] = cos, -sin
        back[:, 1, k, 0, k, :], back[:, 1, k, 1, k, :] = sin, cos
    col_fwd = full.reshape(512, 512)
    col_inv = back.reshape(512, 512)
    half_fwd = np.zeros((2, 192, 2, 144))
    half_inv = np.zeros((2, 144, 2, 192))
    rho = np.arange(ROWS)
    cos, sin = angle(rho[:, None] * rho[None, :], ROWS)
    for j in range(SMALL):
        a = 24 * j + rho[None, :]
        b = 8 * rho[:, None] + j
        half_fwd[0, b, 0, a], half_fwd[0, b, 1, a] = cos, sin
        half_fwd[1, b, 0, a], half_fwd[1, b, 1, a] = -sin, cos
        half_inv[0, a, 0, b], half_inv[0, a, 1, b] = cos, -sin
        half_inv[1, a, 0, b], half_inv[1, a, 1, b] = sin, cos
    half_fwd = half_fwd.reshape(384, 288)
    half_inv = half_inv.reshape(288, 384)
    cos, sin = angle(np.arange(SMALL)[:, None] * samp[None, :], N)
    row_tw = np.zeros((2, 8, BIG))
    row_tw[0, :SMALL], row_tw[1, :SMALL] = cos, sin
    cos, sin = angle(rho[:, None] * m64[None, :], N)
    col_tw = np.stack([np.tile(cos, (1, KEEP)), np.tile(sin, (1, KEEP))])
    mats = np.stack([row_fwd, col_fwd.T, col_inv, row_inv])
    f32 = lambda a: np.asarray(a, np.float32)
    return bf(mats), bf(half_fwd), bf(half_inv), f32(row_tw), f32(col_tw)


def dot(a, b, dims=((1,), (0,))):
    return lax.dot_general(a, b, (dims, ((), ())), preferred_element_type=F32)


def dft_three(x, orient):
    (ar, ai), (br, bi), (cr, ci) = x
    tr, ti = br + cr, bi + ci
    er, ei = (br - cr) * (orient * math.sqrt(0.75)), (bi - ci) * (orient * math.sqrt(0.75))
    mr, mi = ar - 0.5 * tr, ai - 0.5 * ti
    return (ar + tr, ai + ti), (mr + ei, mi - er), (mr - ei, mi + er)


def dft_six(x, orient):
    out = [None] * 6
    for k1 in range(2):
        sums = []
        for n2 in range(3):
            (ar, ai), (br, bi) = x[(2 * n2) % 6], x[(3 + 2 * n2) % 6]
            sums.append((ar + br, ai + bi) if k1 == 0 else (ar - br, ai - bi))
        three = dft_three(sums, orient)
        for k2 in range(3):
            out[(3 * k1 + 4 * k2) % 6] = three[k2]
    return out


def pack(y, main, rest, fold):
    main[...] = y[:, :128].reshape(SLABS, 8, 128).astype(BF16)
    fold[...] = y[:, 128:]
    row = fold[pl.ds(0, SLABS, stride=8), :]
    for i in range(1, 8):
        row = row + pltpu.roll(fold[pl.ds(i, SLABS, stride=8), :], 16 * i, 1)
    rest[...] = row.reshape(SLABS, 1, 128)


def unpack(main, rest, fold):
    row = rest[...].reshape(SLABS, 128)
    fold[pl.ds(0, SLABS, stride=8), :] = row
    for i in range(1, 8):
        fold[pl.ds(i, SLABS, stride=8), :] = pltpu.roll(row, 128 - 16 * i, 1)
    both = [main[...].astype(F32).reshape(512, 128), fold[...]]
    return jnp.concatenate(both, axis=1).astype(BF16)


def hop(a, n):
    return min(a, n - a)


def slab_order():
    offs = [(y, z, c) for y in range(4) for z in range(8) for c in range(2)][1:]
    offs.sort(key=lambda t: (-(hop(t[0], 4) + hop(t[1], 8)), t[2], t[1], t[0]))
    plus = [t for t in offs if 0 < t[1] < 4]
    minus = [t for t in offs if t[1] > 4]
    rest = [t for t in offs if t[1] in (0, 4)]
    out = []
    for i in range(len(plus)):
        out += [plus[i], minus[i]] + rest[i : i + 1]
    return out + rest[len(plus) :]


def kernel(inc_hbm, trans_hbm, phase_hbm, cot_hbm, mats_hbm, half_fwd_hbm, half_inv_hbm, row_tw_hbm,
           col_tw_hbm, out, field, phase, mats, half_fwd, half_inv, row_tw, col_tw,
           tbuf, cur, zbuf, fold, send1, send1r, recv1, recv1r, send2, send2r, recv2, recv2r,
           recv3, recv3r, results, hbuf, outgoing,
           load, load_mat, a2a_send, a2a_recv, t_send, t_recv, r_send, r_recv):
    depth = lax.axis_index("depth")
    slab = lax.axis_index("slab")
    y0, z0, c0 = slab // 16, (slab // 2) % 8, slab % 2
    forward = depth >= 2
    adjoint = depth < 2
    which_field = lax.rem(depth, 2)
    partners = [
        lax.rem(y0 + dy, 4) * 16 + lax.rem(z0 + dz, 8) * 2 + lax.rem(c0 + dc, 2)
        for dy, dz, dc in slab_order()
    ]
    others = [lax.rem(depth + o, DEPTH) for o in range(1, DEPTH)]

    barrier = pltpu.get_barrier_semaphore()
    for p in partners:
        pl.semaphore_signal(barrier, inc=1, device_id=(depth, p), device_id_type=MESH)
    for d in others:
        pl.semaphore_signal(barrier, inc=1, device_id=(d, slab), device_id_type=MESH)

    @pl.when(adjoint)
    def _():
        pltpu.make_async_copy(cot_hbm.at[which_field], field, load.at[0]).start()

    @pl.when(forward)
    def _():
        pltpu.make_async_copy(inc_hbm.at[which_field], field, load.at[0]).start()

    loads = [
        pltpu.make_async_copy(row_tw_hbm, row_tw, load.at[1]),
        pltpu.make_async_copy(col_tw_hbm, col_tw, load.at[2]),
        pltpu.make_async_copy(phase_hbm, phase, load.at[3]),
        pltpu.make_async_copy(trans_hbm, tbuf.at[depth], load.at[4]),
    ]
    mat_loads = [pltpu.make_async_copy(mats_hbm.at[k], mats.at[k], load_mat.at[k]) for k in range(4)]
    mat_loads.append(pltpu.make_async_copy(half_fwd_hbm, half_fwd, load_mat.at[4]))
    mat_loads.append(pltpu.make_async_copy(half_inv_hbm, half_inv, load_mat.at[5]))
    loads[0].start()
    mat_loads[0].start()
    for copy in loads[1:] + mat_loads[1:]:
        copy.start()

    @pl.when(depth == 0)
    def _():
        for m in range(2):
            pltpu.make_async_copy(inc_hbm.at[m], results.at[2 + m], load.at[5 + m]).start()

    zbuf[144:, :] = jnp.zeros((112, 512), F32)
    hbuf[0] = jnp.zeros((192, 256), F32)
    orient = jnp.where(forward, 1.0, -1.0).astype(F32)

    def t_copy(d):
        return pltpu.make_async_remote_copy(
            src_ref=trans_hbm, dst_ref=tbuf.at[depth], send_sem=t_send.at[d], recv_sem=t_recv.at[depth],
            device_id=(d, slab), device_id_type=MESH)

    def t_needed(source, target):
        return jnp.where(target < 2, source >= 1, source <= 2)

    def t_arrived(which):
        @pl.when(which != depth)
        def _():
            pltpu.make_async_copy(field, tbuf.at[which], t_recv.at[which]).wait()

    def multiply(values, which):
        f = values.astype(F32)
        t = tbuf[which].astype(F32)
        fr, fi, tr, ti = f[:ROWS], f[ROWS:], t[:ROWS], t[ROWS:] * orient
        cur[:ROWS] = (fr * tr - fi * ti).astype(BF16).astype(F32)
        cur[ROWS:] = (fr * ti + fi * tr).astype(BF16).astype(F32)

    def send_to(which, plane, p, sent, sent_rest, received, received_rest):
        pltpu.make_async_remote_copy(
            src_ref=sent.at[p], dst_ref=received.at[slab], send_sem=a2a_send.at[which, 0],
            recv_sem=a2a_recv.at[which, 0], device_id=(plane, p), device_id_type=MESH).start()
        pltpu.make_async_remote_copy(
            src_ref=sent_rest.at[p], dst_ref=received_rest.at[slab], send_sem=a2a_send.at[which, 1],
            recv_sem=a2a_recv.at[which, 1], device_id=(plane, p), device_id_type=MESH).start()

    def exchange(which, sent, sent_rest, received, received_rest):
        for p in partners:
            send_to(which, depth, p, sent, sent_rest, received, received_rest)
        received[slab] = sent[slab]
        received_rest[slab] = sent_rest[slab]

    def wait_all(sem, which, count, main, rest):
        for k, ref in enumerate((main, rest)):
            part = ref.at[pl.ds(0, count)]
            pltpu.make_async_copy(part, part, sem.at[which, k]).wait()

    def stage_a():
        for half in range(2):
            lo = 128 * half
            x = [(cur[:ROWS, BIG * a + lo : BIG * a + lo + 128], cur[ROWS:, BIG * a + lo : BIG * a + lo + 128])
                 for a in range(SMALL)]
            for j, (zr, zi) in enumerate(dft_six(x, 1.0)):
                c = row_tw[0, j : j + 1, lo : lo + 128]
                s = row_tw[1, j : j + 1, lo : lo + 128]
                zbuf[ROWS * j : ROWS * j + ROWS, lo : lo + 128] = zr * c + zi * s
                zbuf[ROWS * j : ROWS * j + ROWS, BIG + lo : BIG + lo + 128] = zi * c - zr * s
        pack(dot(mats[0], zbuf[...].astype(BF16), ((1,), (1,))), send1, send1r, fold)

    def make_filter():
        for p in range(ROWS):
            lo = 128 * (p // 2)
            for chunk in range(2):
                low = phase[12 * chunk : 12 * chunk + SMALL, lo : lo + 128]
                high = phase[12 * chunk + SMALL : 12 * chunk + 12, lo : lo + 128]
                if p % 2 == 0:
                    high = pltpu.roll(high, 64, 1)
                else:
                    low = pltpu.roll(low, 64, 1)
                lane = lax.broadcasted_iota(jnp.int32, (SMALL, 128), 1)
                angles = jnp.where(lane < 64, low, high)
                hbuf[0, 8 * p : 8 * p + SMALL, 128 * chunk : 128 * chunk + 128] = angles
        angles = hbuf[0]
        hbuf[0] = jnp.cos(angles)
        hbuf[1] = jnp.sin(angles) * orient

    def stage_b():
        y = dot(unpack(recv1, recv1r, fold)[:, :144], mats[1], ((0,), (0,)))
        c, s = col_tw[0], col_tw[1]
        parts = [[], []]
        for j in range(SMALL):
            yr, yi = y[ROWS * j : ROWS * j + ROWS, :256], y[ROWS * j : ROWS * j + ROWS, 256:]
            parts[0].append(yr * c + yi * s)
            parts[1].append(yi * c - yr * s)
        y = dot(half_fwd[...], jnp.concatenate(parts[0] + parts[1], axis=0).astype(BF16))
        yr, yi, hr, hi = y[:192], y[192:], hbuf[0], hbuf[1]
        z = jnp.concatenate([yr * hr - yi * hi, yi * hr + yr * hi], axis=0)
        y = dot(half_inv[...], z.astype(BF16))
        c, s = c * (1.0 / N), s * (1.0 / N)
        for j in range(SMALL):
            yr, yi = y[ROWS * j : ROWS * j + ROWS], y[144 + ROWS * j : 144 + ROWS * j + ROWS]
            zbuf[ROWS * j : ROWS * j + ROWS, :256] = yr * c - yi * s
            zbuf[ROWS * j : ROWS * j + ROWS, 256:] = yi * c + yr * s
        pack(dot(mats[2], zbuf[...].astype(BF16), ((1,), (1,))), send2, send2r, fold)

    def stage_c(main, rest, target, index):
        zbuf_c = dot(unpack(main, rest, fold)[:, :144], mats[3], ((0,), (0,)))
        for half in range(2):
            lo = 128 * half
            x = []
            for j in range(SMALL):
                c = row_tw[0, j : j + 1, lo : lo + 128] * (1.0 / N)
                s = row_tw[1, j : j + 1, lo : lo + 128] * (1.0 / N)
                zr = zbuf_c[ROWS * j : ROWS * j + ROWS, lo : lo + 128]
                zi = zbuf_c[ROWS * j : ROWS * j + ROWS, BIG + lo : BIG + lo + 128]
                x.append((zr * c - zi * s, zi * c + zr * s))
            for a, (vr, vi) in enumerate(dft_six(x, -1.0)):
                both = jnp.concatenate([vr, vi], axis=0)
                target[index, :, BIG * a + lo : BIG * a + lo + 128] = both.astype(BF16)

    def r_copy(turn, target):
        return pltpu.make_async_remote_copy(
            src_ref=outgoing.at[turn], dst_ref=results.at[depth], send_sem=r_send.at[turn],
            recv_sem=r_recv.at[depth], device_id=(target, slab), device_id_type=MESH)

    def target_of(turn):
        return jnp.where(forward, turn + 1, DEPTH - 1 - turn)

    pltpu.make_async_copy(inc_hbm.at[0], field, load.at[0]).wait()
    loads[0].wait()
    mat_loads[0].wait()

    @pl.when(adjoint)
    def _():
        cur[...] = field[...].astype(F32)
        stage_a()

    loads[3].wait()
    loads[2].wait()
    make_filter()
    pl.semaphore_wait(barrier, len(partners) + len(others))

    for d in others:
        @pl.when(t_needed(depth, d))
        def _(d=d):
            t_copy(d).start()

    @pl.when(forward)
    def _():
        t_arrived(0)
        multiply(field[...], 0)
        stage_a()

    for copy in loads[1:2] + mat_loads[1:]:
        copy.wait()

    first = send1, send1r, recv1, recv1r
    second = send2, send2r, recv2, recv2r
    last = DEPTH - 1
    most = SLABS - 1

    @pl.loop(0, DEPTH)
    def _(turn):
        @pl.when(adjoint | (turn < last))
        def _():
            exchange(0, *first)
            wait_all(a2a_recv, 0, most, recv1, recv1r)

            @pl.when(turn > 0)
            def _():
                wait_all(a2a_send, 1, most, send2, send2r)

            stage_b()
            direct = (depth == 1) & (turn == last)

            @pl.when(direct)
            def _():
                pltpu.make_async_copy(field, results.at[0], r_recv.at[0]).wait()
                for p in partners + [slab]:
                    send_to(2, 0, p, send2, send2r, recv3, recv3r)
                wait_all(a2a_send, 0, most, send1, send1r)

            @pl.when(jnp.logical_not(direct))
            def _():
                exchange(1, *second)
                wait_all(a2a_recv, 1, most, recv2, recv2r)
                wait_all(a2a_send, 0, most, send1, send1r)
                stage_c(recv2, recv2r, outgoing, turn)
                target = target_of(turn)

                @pl.when(target != depth)
                def _():
                    r_copy(turn, target).start()

                @pl.when(target == depth)
                def _():
                    results[depth] = outgoing[turn]

                @pl.when(jnp.where(forward, turn < last - 1, turn < last))
                def _():
                    t_arrived(target)
                    multiply(outgoing[turn], target)
                    stage_a()

    @pl.when(depth == 0)
    def _():
        for m in range(2):
            pltpu.make_async_copy(inc_hbm.at[m], results.at[2 + m], load.at[5 + m]).wait()
        wait_all(a2a_recv, 2, SLABS, recv3, recv3r)
        stage_c(recv3, recv3r, results, 1)

    for slot, needed in ((0, depth >= 2), (1, depth >= 2), (2, (depth == 1) | (depth == 3)), (3, (depth == 1) | (depth == 2))):
        @pl.when(needed)
        def _(slot=slot):
            pltpu.make_async_copy(field, results.at[slot], r_recv.at[slot]).wait()

    gr = jnp.zeros((ROWS, N), F32)
    gi = jnp.zeros((ROWS, N), F32)
    for m in range(2):
        u = results[2 + m].astype(F32)
        p = results[m].astype(F32)
        ur, ui, pr, pi = u[:ROWS], u[ROWS:], p[:ROWS], p[ROWS:]
        gr = gr + (ur * pr + ui * pi)
        gi = gi + (ur * pi - ui * pr)
    out[:ROWS] = gr
    out[ROWS:] = gi

    for d in others:
        @pl.when(t_needed(depth, d))
        def _(d=d):
            t_copy(d).wait_send()

    for turn in range(last):
        target = target_of(turn)

        @pl.when(target != depth)
        def _(turn=turn, target=target):
            r_copy(turn, target).wait_send()

    @pl.when(depth == 1)
    def _():
        wait_all(a2a_send, 2, SLABS, send2, send2r)

    @pl.when(depth != 1)
    def _():
        wait_all(a2a_send, 1, most, send2, send2r)


def on_device(incident, transmission, prop_phase, cotangent):
    mats, half_fwd, half_inv, row_tw, col_tw = (jnp.asarray(t) for t in make_tables())
    inc = incident.reshape(2, 2 * ROWS, N)
    trans = transmission.reshape(2 * ROWS, N)
    cot = cotangent.reshape(2, 2 * ROWS, N)
    hbm = pl.BlockSpec(memory_space=pltpu.HBM)
    field = (2 * ROWS, N)
    main = pltpu.VMEM((SLABS, 8, 128), BF16)
    rest = pltpu.VMEM((SLABS, 1, 128), F32)
    dma = pltpu.SemaphoreType.DMA
    grads = pl.pallas_call(
        kernel,
        out_shape=jax.ShapeDtypeStruct(field, F32),
        in_specs=[hbm] * 9,
        out_specs=pl.BlockSpec(memory_space=pltpu.VMEM),
        scratch_shapes=[
            pltpu.VMEM(field, BF16),
            pltpu.VMEM((ROWS, N), F32),
            pltpu.VMEM(mats.shape, BF16),
            pltpu.VMEM(half_fwd.shape, BF16),
            pltpu.VMEM(half_inv.shape, BF16),
            pltpu.VMEM(row_tw.shape, F32),
            pltpu.VMEM(col_tw.shape, F32),
            pltpu.VMEM((DEPTH,) + field, BF16),
            pltpu.VMEM(field, F32),
            pltpu.VMEM((256, 512), F32),
            pltpu.VMEM((512, 128), F32),
            main, rest, main, rest, main, rest, main, rest, main, rest,
            pltpu.VMEM((DEPTH,) + field, BF16),
            pltpu.VMEM((2, 192, 256), F32),
            pltpu.VMEM((DEPTH,) + field, BF16),
            dma((7,)), dma((6,)), dma((3, 2)), dma((3, 2)),
            dma((DEPTH,)), dma((DEPTH,)), dma((DEPTH,)), dma((DEPTH,)),
        ],
        compiler_params=pltpu.CompilerParams(
            collective_id=0, has_side_effects=True, vmem_limit_bytes=62 * 2**20),
        name="chains",
    )(inc, trans, prop_phase.T, cot, mats, half_fwd, half_inv, row_tw, col_tw)
    return grads.reshape(1, 2, ROWS, N)


def solution(mesh):
    in_specs = (
        P(None, None, "slab", None),
        P("depth", None, "slab", None),
        P(None, "slab"),
        P(None, None, "slab", None),
    )
    out_specs = P("depth", None, "slab", None)
    return jax.shard_map(
        on_device, mesh=mesh, in_specs=in_specs, out_specs=out_specs, check_vma=False
    )
```

```python
import functools
import math

import jax
import jax.numpy as jnp
import numpy as np
from jax import lax
from jax.experimental import pallas as pl
from jax.experimental.pallas import tpu as pltpu
from jax.sharding import PartitionSpec as P

N = 1536
SLABS = 64
ROWS = N // SLABS
BIG = 256
SMALL = N // BIG
KEEP = BIG // SLABS
DEPTH = 4
GROUP = SMALL // 2
MESH = pl.DeviceIdType.MESH
F32 = jnp.float32
BF16 = jnp.bfloat16


def angle(x, period):
    turn = 2.0 * math.pi * (x % period) / period
    return np.cos(turn), np.sin(turn)


def block_matrix(re_re, re_im, im_re, im_im):
    return np.block([[re_re, re_im], [im_re, im_im]])


@functools.lru_cache(None)
def make_tables():
    bf = lambda a: np.asarray(a, np.float32).astype(jnp.bfloat16)
    freq = np.arange(BIG)
    samp = np.arange(BIG)
    cos, sin = angle(freq[:, None] * samp[None, :], BIG)
    cos = cos.reshape(SLABS, 2, 2, BIG).transpose(1, 2, 0, 3)
    sin = sin.reshape(SLABS, 2, 2, BIG).transpose(1, 2, 0, 3)
    full = np.zeros((2, 2, 2, SLABS, 2, BIG))
    full[:, 0, :, :, 0], full[:, 0, :, :, 1] = cos, sin
    full[:, 1, :, :, 0], full[:, 1, :, :, 1] = -sin, cos
    rows = full.reshape(512, 512)
    m64 = np.arange(SLABS)
    cos, sin = angle(m64[:, None] * m64[None, :], SLABS)
    full = np.zeros((2, 2, SLABS, 2, 2, SLABS))
    back = np.zeros((2, 2, SLABS, 2, 2, SLABS))
    for k in range(2):
        full[0, k, :, 0, k], full[1, k, :, 0, k] = cos, sin
        full[0, k, :, 1, k], full[1, k, :, 1, k] = -sin, cos
        back[0, k, :, 0, k], back[0, k, :, 1, k] = cos, -sin
        back[1, k, :, 0, k], back[1, k, :, 1, k] = sin, cos
    cols = np.stack([full.reshape(256, 256), back.reshape(256, 256)])
    half_fwd = np.zeros((2, 96, 2, 72))
    half_inv = np.zeros((2, 72, 2, 96))
    rho = np.arange(ROWS)
    cos, sin = angle(rho[:, None] * rho[None, :], ROWS)
    for j in range(GROUP):
        a = 24 * j + rho[None, :]
        b = 4 * rho[:, None] + j
        half_fwd[0, b, 0, a], half_fwd[0, b, 1, a] = cos, sin
        half_fwd[1, b, 0, a], half_fwd[1, b, 1, a] = -sin, cos
        half_inv[0, a, 0, b], half_inv[0, a, 1, b] = cos, -sin
        half_inv[1, a, 0, b], half_inv[1, a, 1, b] = sin, cos
    half_fwd = half_fwd.reshape(192, 144)
    half_inv = half_inv.reshape(144, 192)
    cos, sin = angle(np.arange(SMALL)[:, None] * samp[None, :], N)
    row_tw = np.zeros((2, 8, BIG))
    row_tw[0, :SMALL], row_tw[1, :SMALL] = cos, sin
    cos, sin = angle(rho[:, None] * m64[None, :], N)
    col_tw = np.stack([np.tile(cos, (1, 2)), np.tile(sin, (1, 2))])
    f32 = lambda a: np.asarray(a, np.float32)
    return bf(rows), bf(cols), bf(half_fwd), bf(half_inv), f32(row_tw), f32(col_tw)


def dot(a, b, dims=((1,), (0,))):
    return lax.dot_general(a, b, (dims, ((), ())), preferred_element_type=F32)


def dft_three(x, orient):
    (ar, ai), (br, bi), (cr, ci) = x
    tr, ti = br + cr, bi + ci
    er, ei = (br - cr) * (orient * math.sqrt(0.75)), (bi - ci) * (orient * math.sqrt(0.75))
    mr, mi = ar - 0.5 * tr, ai - 0.5 * ti
    return (ar + tr, ai + ti), (mr + ei, mi - er), (mr - ei, mi + er)


def dft_six(x, orient):
    out = [None] * 6
    for k1 in range(2):
        sums = []
        for n2 in range(3):
            (ar, ai), (br, bi) = x[(2 * n2) % 6], x[(3 + 2 * n2) % 6]
            sums.append((ar + br, ai + bi) if k1 == 0 else (ar - br, ai - bi))
        three = dft_three(sums, orient)
        for k2 in range(3):
            out[(3 * k1 + 4 * k2) % 6] = three[k2]
    return out


def pack(y, first, row, fold):
    for i in range(y.shape[0] // SLABS):
        block = y[SLABS * i : SLABS * i + SLABS]
        fold[pl.ds(first + i, SLABS, stride=8), :] = block[:, :128]
        tail = block[:, 128:]
        if first + i > 0:
            tail = pltpu.roll(tail, 16 * (first + i), 1)
        row = tail if row is None else row + tail
    return row


def finish_pack(row, main, rest, fold):
    main[...] = fold[...].reshape(SLABS, 8, 128).astype(BF16)
    rest[...] = row.reshape(SLABS, 1, 128)


def unpack(main, rest, fold):
    fold[...] = main[...].astype(F32).reshape(512, 128)
    row = rest[...].reshape(SLABS, 128)
    blocks = []
    for i in range(8):
        tail = pltpu.roll(row, 128 - 16 * i, 1) if i else row
        blocks.append(jnp.concatenate([fold[pl.ds(i, SLABS, stride=8), :], tail], axis=1))
    return jnp.concatenate(blocks, axis=0).astype(BF16)


def hop(a, n):
    return min(a, n - a)


def slab_order():
    offs = [(y, z, c) for y in range(4) for z in range(8) for c in range(2)][1:]
    offs.sort(key=lambda t: (-(hop(t[0], 4) + hop(t[1], 8)), t[2], t[1], t[0]))
    plus = [t for t in offs if 0 < t[1] < 4]
    minus = [t for t in offs if t[1] > 4]
    rest = [t for t in offs if t[1] in (0, 4)]
    out = []
    for i in range(len(plus)):
        out += [plus[i], minus[i]] + rest[i : i + 1]
    return out + rest[len(plus) :]


def final_order():
    slabs = [(y * 16 + z * 2 + c, z) for z in range(8) for y in range(4) for c in range(2)]
    slabs.sort(key=lambda t: (t[0] != 1, t[1] != 0))
    head, tail = slabs[:1], slabs[1:]
    tail.sort(key=lambda t: (t[0] * 29) % 64)
    return [p for p, _ in head + tail]


def kernel(inc_hbm, trans_hbm, phase_hbm, cot_hbm, rows_hbm, cols_hbm, half_fwd_hbm, half_inv_hbm, row_tw_hbm,
           col_tw_hbm, out, field, phase, rows, cols, half_fwd, half_inv, row_tw, col_tw,
           tbuf, cur, zbuf, zcol, fold, send1, send1r, recv1, recv1r, send2, send2r, recv2, recv2r,
           recv3, recv3r, results, hbuf, outgoing,
           load, load_mat, a2a_send, a2a_recv, t_send, t_recv, r_send, r_recv):
    depth = lax.axis_index("depth")
    slab = lax.axis_index("slab")
    y0, z0, c0 = slab // 16, (slab // 2) % 8, slab % 2
    forward = depth >= 2
    adjoint = depth < 2
    which_field = lax.rem(depth, 2)
    partners = [
        lax.rem(y0 + dy, 4) * 16 + lax.rem(z0 + dz, 8) * 2 + lax.rem(c0 + dc, 2)
        for dy, dz, dc in slab_order()
    ]
    others = [lax.rem(depth + o, DEPTH) for o in range(1, DEPTH)]

    barrier = pltpu.get_barrier_semaphore()
    for p in partners:
        pl.semaphore_signal(barrier, inc=1, device_id=(depth, p), device_id_type=MESH)
    for d in others:
        pl.semaphore_signal(barrier, inc=1, device_id=(d, slab), device_id_type=MESH)

    @pl.when(adjoint)
    def _():
        pltpu.make_async_copy(cot_hbm.at[which_field], field, load.at[0]).start()

    @pl.when(forward)
    def _():
        pltpu.make_async_copy(inc_hbm.at[which_field], field, load.at[0]).start()

    loads = [
        pltpu.make_async_copy(row_tw_hbm, row_tw, load.at[1]),
        pltpu.make_async_copy(col_tw_hbm, col_tw, load.at[2]),
        pltpu.make_async_copy(phase_hbm, phase, load.at[3]),
        pltpu.make_async_copy(trans_hbm, tbuf.at[depth], load.at[4]),
    ]
    mat_loads = [
        pltpu.make_async_copy(rows_hbm, rows, load_mat.at[0]),
        pltpu.make_async_copy(cols_hbm, cols, load_mat.at[1]),
        pltpu.make_async_copy(half_fwd_hbm, half_fwd, load_mat.at[2]),
        pltpu.make_async_copy(half_inv_hbm, half_inv, load_mat.at[3]),
    ]
    loads[0].start()
    mat_loads[0].start()
    for copy in loads[1:] + mat_loads[1:]:
        copy.start()

    @pl.when(depth == 0)
    def _():
        for m in range(2):
            pltpu.make_async_copy(inc_hbm.at[m], results.at[2 + m], load.at[5 + m]).start()

    zbuf[144:, :] = jnp.zeros((112, 512), F32)
    zcol[:, 144:, :] = jnp.zeros((2, 112, 256), F32)
    hbuf[0] = jnp.zeros((2, 96, 256), F32)
    orient = jnp.where(forward, 1.0, -1.0).astype(F32)

    def t_copy(d):
        return pltpu.make_async_remote_copy(
            src_ref=trans_hbm, dst_ref=tbuf.at[depth], send_sem=t_send.at[d], recv_sem=t_recv.at[depth],
            device_id=(d, slab), device_id_type=MESH)

    def t_needed(source, target):
        return jnp.where(target < 2, source >= 1, source <= 2)

    def t_arrived(which):
        @pl.when(which != depth)
        def _():
            pltpu.make_async_copy(field, tbuf.at[which], t_recv.at[which]).wait()

    def multiply(values, which):
        f = values.astype(F32)
        t = tbuf[which].astype(F32)
        fr, fi, tr, ti = f[:ROWS], f[ROWS:], t[:ROWS], t[ROWS:] * orient
        cur[:ROWS] = (fr * tr - fi * ti).astype(BF16).astype(F32)
        cur[ROWS:] = (fr * ti + fi * tr).astype(BF16).astype(F32)

    def send_to(which, plane, p, sent, sent_rest, received, received_rest):
        pltpu.make_async_remote_copy(
            src_ref=sent.at[p], dst_ref=received.at[slab], send_sem=a2a_send.at[which, 0],
            recv_sem=a2a_recv.at[which, 0], device_id=(plane, p), device_id_type=MESH).start()
        pltpu.make_async_remote_copy(
            src_ref=sent_rest.at[p], dst_ref=received_rest.at[slab], send_sem=a2a_send.at[which, 1],
            recv_sem=a2a_recv.at[which, 1], device_id=(plane, p), device_id_type=MESH).start()

    def exchange(which, sent, sent_rest, received, received_rest):
        for p in partners:
            send_to(which, depth, p, sent, sent_rest, received, received_rest)
        received[slab] = sent[slab]
        received_rest[slab] = sent_rest[slab]

    def wait_all(sem, which, count, main, rest):
        for k, ref in enumerate((main, rest)):
            part = ref.at[pl.ds(0, count)]
            pltpu.make_async_copy(part, part, sem.at[which, k]).wait()

    def stage_a():
        for half in range(2):
            lo = 128 * half
            x = [(cur[:ROWS, BIG * a + lo : BIG * a + lo + 128], cur[ROWS:, BIG * a + lo : BIG * a + lo + 128])
                 for a in range(SMALL)]
            for j, (zr, zi) in enumerate(dft_six(x, 1.0)):
                c = row_tw[0, j : j + 1, lo : lo + 128]
                s = row_tw[1, j : j + 1, lo : lo + 128]
                zbuf[ROWS * j : ROWS * j + ROWS, lo : lo + 128] = zr * c + zi * s
                zbuf[ROWS * j : ROWS * j + ROWS, BIG + lo : BIG + lo + 128] = zi * c - zr * s
        row = pack(dot(rows[...], zbuf[...].astype(BF16), ((1,), (1,))), 0, None, fold)
        finish_pack(row, send1, send1r, fold)

    def make_filter():
        lane = lax.broadcasted_iota(jnp.int32, (SMALL, 128), 1)
        for p in range(ROWS):
            lo = 128 * (p // 2)
            for h in range(2):
                low = phase[12 * h : 12 * h + SMALL, lo : lo + 128]
                high = phase[12 * h + SMALL : 12 * h + 12, lo : lo + 128]
                if p % 2 == 0:
                    high = pltpu.roll(high, 64, 1)
                else:
                    low = pltpu.roll(low, 64, 1)
                angles = jnp.where(lane < 64, low, high)
                for g in range(2):
                    hbuf[0, h, 4 * p : 4 * p + GROUP, 128 * g : 128 * g + 128] = (
                        angles[GROUP * g : GROUP * g + GROUP])
        angles = hbuf[0]
        hbuf[0] = jnp.cos(angles)
        hbuf[1] = jnp.sin(angles) * orient

    def stage_b():
        x = unpack(recv1, recv1r, fold)[:, :144]
        c, s = col_tw[0], col_tw[1]
        cs, ss = c * (1.0 / N), s * (1.0 / N)
        halves = [dot(x[256 * h : 256 * h + 256], cols[0], ((0,), (0,))) for h in range(2)]
        for h, y in enumerate(halves):
            parts = [[], []]
            for i in range(GROUP):
                wide = [[], []]
                for g in range(2):
                    j = GROUP * g + i
                    yr, yi = y[ROWS * j : ROWS * j + ROWS, :128], y[ROWS * j : ROWS * j + ROWS, 128:]
                    wide[0].append(yr * c + yi * s)
                    wide[1].append(yi * c - yr * s)
                parts[0].append(jnp.concatenate(wide[0], axis=1))
                parts[1].append(jnp.concatenate(wide[1], axis=1))
            halves[h] = jnp.concatenate(parts[0] + parts[1], axis=0).astype(BF16)
        halves = [dot(half_fwd[...], x) for x in halves]
        for h, x in enumerate(halves):
            xr, xi, hr, hi = x[:96], x[96:], hbuf[0, h], hbuf[1, h]
            halves[h] = jnp.concatenate([xr * hr - xi * hi, xi * hr + xr * hi], axis=0).astype(BF16)
        halves = [dot(half_inv[...], x) for x in halves]
        for h, x in enumerate(halves):
            for i in range(GROUP):
                for g in range(2):
                    j = GROUP * g + i
                    xr = x[ROWS * i : ROWS * i + ROWS, 128 * g : 128 * g + 128]
                    xi = x[72 + ROWS * i : 72 + ROWS * i + ROWS, 128 * g : 128 * g + 128]
                    zcol[h, ROWS * j : ROWS * j + ROWS, :128] = xr * cs - xi * ss
                    zcol[h, ROWS * j : ROWS * j + ROWS, 128:] = xi * cs + xr * ss
        halves = [dot(cols[1], zcol[h].astype(BF16), ((1,), (1,))) for h in range(2)]
        row = None
        for h, y in enumerate(halves):
            row = pack(y, 4 * h, row, fold)
        finish_pack(row, send2, send2r, fold)

    def stage_c(main, rest, target, index):
        zbuf_c = dot(unpack(main, rest, fold)[:, :144], rows[...], ((0,), (0,)))
        for half in range(2):
            lo = 128 * half
            x = []
            for j in range(SMALL):
                c = row_tw[0, j : j + 1, lo : lo + 128] * (1.0 / N)
                s = row_tw[1, j : j + 1, lo : lo + 128] * (1.0 / N)
                zr = zbuf_c[ROWS * j : ROWS * j + ROWS, lo : lo + 128]
                zi = zbuf_c[ROWS * j : ROWS * j + ROWS, BIG + lo : BIG + lo + 128]
                x.append((zr * c - zi * s, zi * c + zr * s))
            for a, (vr, vi) in enumerate(dft_six(x, -1.0)):
                both = jnp.concatenate([vr, vi], axis=0)
                target[index, :, BIG * a + lo : BIG * a + lo + 128] = both.astype(BF16)

    def r_copy(turn, target):
        return pltpu.make_async_remote_copy(
            src_ref=outgoing.at[turn], dst_ref=results.at[depth], send_sem=r_send.at[turn],
            recv_sem=r_recv.at[depth], device_id=(target, slab), device_id_type=MESH)

    def target_of(turn):
        return jnp.where(forward, turn + 1, DEPTH - 1 - turn)

    pltpu.make_async_copy(inc_hbm.at[0], field, load.at[0]).wait()
    loads[0].wait()
    mat_loads[0].wait()

    @pl.when(adjoint)
    def _():
        cur[...] = field[...].astype(F32)
        stage_a()

    loads[3].wait()
    loads[2].wait()
    make_filter()
    pl.semaphore_wait(barrier, len(partners) + len(others))

    for d in others:
        @pl.when(t_needed(depth, d))
        def _(d=d):
            t_copy(d).start()

    @pl.when(forward)
    def _():
        t_arrived(0)
        multiply(field[...], 0)
        stage_a()

    for copy in loads[1:2] + mat_loads[1:]:
        copy.wait()

    first = send1, send1r, recv1, recv1r
    second = send2, send2r, recv2, recv2r
    last = DEPTH - 1
    most = SLABS - 1

    @pl.loop(0, DEPTH)
    def _(turn):
        @pl.when(adjoint | (turn < last))
        def _():
            exchange(0, *first)
            wait_all(a2a_recv, 0, most, recv1, recv1r)

            @pl.when(turn > 0)
            def _():
                wait_all(a2a_send, 1, most, send2, send2r)

            stage_b()
            direct = (depth == 1) & (turn == last)

            @pl.when(direct)
            def _():
                pltpu.make_async_copy(field, results.at[0], r_recv.at[0]).wait()
                for p in final_order():
                    send_to(2, 0, p, send2, send2r, recv3, recv3r)
                wait_all(a2a_send, 0, most, send1, send1r)

            @pl.when(jnp.logical_not(direct))
            def _():
                @pl.when(turn < last)
                def _():
                    exchange(1, *second)

                @pl.when(turn == last)
                def _():
                    for p in final_order():
                        @pl.when(p != slab)
                        def _(p=p):
                            send_to(1, 0, p, *second)
                    recv2[slab] = send2[slab]
                    recv2r[slab] = send2r[slab]

                wait_all(a2a_recv, 1, most, recv2, recv2r)
                wait_all(a2a_send, 0, most, send1, send1r)
                stage_c(recv2, recv2r, outgoing, turn)
                target = target_of(turn)

                @pl.when(target != depth)
                def _():
                    r_copy(turn, target).start()

                @pl.when(target == depth)
                def _():
                    results[depth] = outgoing[turn]

                @pl.when(jnp.where(forward, turn < last - 1, turn < last))
                def _():
                    t_arrived(target)
                    multiply(outgoing[turn], target)
                    stage_a()

    @pl.when(depth == 0)
    def _():
        for m in range(2):
            pltpu.make_async_copy(inc_hbm.at[m], results.at[2 + m], load.at[5 + m]).wait()
        wait_all(a2a_recv, 2, SLABS, recv3, recv3r)
        stage_c(recv3, recv3r, results, 1)

    for slot, needed in ((0, depth >= 2), (1, depth >= 2), (2, (depth == 1) | (depth == 3)), (3, (depth == 1) | (depth == 2))):
        @pl.when(needed)
        def _(slot=slot):
            pltpu.make_async_copy(field, results.at[slot], r_recv.at[slot]).wait()

    gr = jnp.zeros((ROWS, N), F32)
    gi = jnp.zeros((ROWS, N), F32)
    for m in range(2):
        u = results[2 + m].astype(F32)
        p = results[m].astype(F32)
        ur, ui, pr, pi = u[:ROWS], u[ROWS:], p[:ROWS], p[ROWS:]
        gr = gr + (ur * pr + ui * pi)
        gi = gi + (ur * pi - ui * pr)
    out[:ROWS] = gr
    out[ROWS:] = gi

    for d in others:
        @pl.when(t_needed(depth, d))
        def _(d=d):
            t_copy(d).wait_send()

    for turn in range(last):
        target = target_of(turn)

        @pl.when(target != depth)
        def _(turn=turn, target=target):
            r_copy(turn, target).wait_send()

    @pl.when(depth == 1)
    def _():
        wait_all(a2a_send, 2, SLABS, send2, send2r)

    @pl.when(depth != 1)
    def _():
        wait_all(a2a_send, 1, most, send2, send2r)


def on_device(incident, transmission, prop_phase, cotangent):
    rows, cols, half_fwd, half_inv, row_tw, col_tw = (jnp.asarray(t) for t in make_tables())
    inc = incident.reshape(2, 2 * ROWS, N)
    trans = transmission.reshape(2 * ROWS, N)
    cot = cotangent.reshape(2, 2 * ROWS, N)
    hbm = pl.BlockSpec(memory_space=pltpu.HBM)
    field = (2 * ROWS, N)
    main = pltpu.VMEM((SLABS, 8, 128), BF16)
    rest = pltpu.VMEM((SLABS, 1, 128), F32)
    dma = pltpu.SemaphoreType.DMA
    grads = pl.pallas_call(
        kernel,
        out_shape=jax.ShapeDtypeStruct(field, F32),
        in_specs=[hbm] * 10,
        out_specs=pl.BlockSpec(memory_space=pltpu.VMEM),
        scratch_shapes=[
            pltpu.VMEM(field, BF16),
            pltpu.VMEM((ROWS, N), F32),
            pltpu.VMEM(rows.shape, BF16),
            pltpu.VMEM(cols.shape, BF16),
            pltpu.VMEM(half_fwd.shape, BF16),
            pltpu.VMEM(half_inv.shape, BF16),
            pltpu.VMEM(row_tw.shape, F32),
            pltpu.VMEM(col_tw.shape, F32),
            pltpu.VMEM((DEPTH,) + field, BF16),
            pltpu.VMEM(field, F32),
            pltpu.VMEM((256, 512), F32),
            pltpu.VMEM((2, 256, 256), F32),
            pltpu.VMEM((512, 128), F32),
            main, rest, main, rest, main, rest, main, rest, main, rest,
            pltpu.VMEM((DEPTH,) + field, BF16),
            pltpu.VMEM((2, 2, 96, 256), F32),
            pltpu.VMEM((DEPTH,) + field, BF16),
            dma((7,)), dma((4,)), dma((3, 2)), dma((3, 2)),
            dma((DEPTH,)), dma((DEPTH,)), dma((DEPTH,)), dma((DEPTH,)),
        ],
        compiler_params=pltpu.CompilerParams(
            collective_id=0, has_side_effects=True, vmem_limit_bytes=62 * 2**20),
        name="chains",
    )(inc, trans, prop_phase.T, cot, rows, cols, half_fwd, half_inv, row_tw, col_tw)
    return grads.reshape(1, 2, ROWS, N)


def solution(mesh):
    in_specs = (
        P(None, None, "slab", None),
        P("depth", None, "slab", None),
        P(None, "slab"),
        P(None, None, "slab", None),
    )
    out_specs = P("depth", None, "slab", None)
    return jax.shard_map(
        on_device, mesh=mesh, in_specs=in_specs, out_specs=out_specs, check_vma=False
    )
```

```python
import functools
import math

import jax
import jax.numpy as jnp
import numpy as np
from jax import lax
from jax.experimental import pallas as pl
from jax.experimental.pallas import tpu as pltpu
from jax.sharding import PartitionSpec as P

N = 1536
SLABS = 64
ROWS = N // SLABS
BIG = 256
SMALL = N // BIG
KEEP = BIG // SLABS
DEPTH = 4
GROUP = SMALL // 2
EARLY = (1, 2, 17, 4, 3, 19, 33, 48, 35, 16)
MESH = pl.DeviceIdType.MESH
F32 = jnp.float32
BF16 = jnp.bfloat16


def angle(x, period):
    turn = 2.0 * math.pi * (x % period) / period
    return np.cos(turn), np.sin(turn)


def block_matrix(re_re, re_im, im_re, im_im):
    return np.block([[re_re, re_im], [im_re, im_im]])


@functools.lru_cache(None)
def make_tables():
    bf = lambda a: np.asarray(a, np.float32).astype(jnp.bfloat16)
    freq = np.arange(BIG)
    samp = np.arange(BIG)
    cos, sin = angle(freq[:, None] * samp[None, :], BIG)
    cos = cos.reshape(SLABS, 2, 2, BIG).transpose(1, 2, 0, 3)
    sin = sin.reshape(SLABS, 2, 2, BIG).transpose(1, 2, 0, 3)
    full = np.zeros((2, 2, 2, SLABS, 2, BIG))
    full[:, 0, :, :, 0], full[:, 0, :, :, 1] = cos, sin
    full[:, 1, :, :, 0], full[:, 1, :, :, 1] = -sin, cos
    rows = full.reshape(512, 512)
    m64 = np.arange(SLABS)
    cos, sin = angle(m64[:, None] * m64[None, :], SLABS)
    full = np.zeros((2, 2, SLABS, 2, 2, SLABS))
    back = np.zeros((2, 2, SLABS, 2, 2, SLABS))
    for k in range(2):
        full[0, k, :, 0, k], full[1, k, :, 0, k] = cos, sin
        full[0, k, :, 1, k], full[1, k, :, 1, k] = -sin, cos
        back[0, k, :, 0, k], back[0, k, :, 1, k] = cos, -sin
        back[1, k, :, 0, k], back[1, k, :, 1, k] = sin, cos
    cols = np.stack([full.reshape(256, 256), back.reshape(256, 256)])
    half_fwd = np.zeros((2, 96, 2, 72))
    half_inv = np.zeros((2, 72, 2, 96))
    rho = np.arange(ROWS)
    cos, sin = angle(rho[:, None] * rho[None, :], ROWS)
    for j in range(GROUP):
        a = 24 * j + rho[None, :]
        b = 4 * rho[:, None] + j
        half_fwd[0, b, 0, a], half_fwd[0, b, 1, a] = cos, sin
        half_fwd[1, b, 0, a], half_fwd[1, b, 1, a] = -sin, cos
        half_inv[0, a, 0, b], half_inv[0, a, 1, b] = cos, -sin
        half_inv[1, a, 0, b], half_inv[1, a, 1, b] = sin, cos
    half_fwd = half_fwd.reshape(192, 144)
    half_inv = half_inv.reshape(144, 192)
    cos, sin = angle(np.arange(SMALL)[:, None] * samp[None, :], N)
    row_tw = np.zeros((2, 8, BIG))
    row_tw[0, :SMALL], row_tw[1, :SMALL] = cos, sin
    cos, sin = angle(rho[:, None] * m64[None, :], N)
    col_tw = np.stack([np.tile(cos, (1, 2)), np.tile(sin, (1, 2))])
    f32 = lambda a: np.asarray(a, np.float32)
    return bf(rows), bf(cols), bf(half_fwd), bf(half_inv), f32(row_tw), f32(col_tw)


def dot(a, b, dims=((1,), (0,))):
    return lax.dot_general(a, b, (dims, ((), ())), preferred_element_type=F32)


def dft_three(x, orient):
    (ar, ai), (br, bi), (cr, ci) = x
    tr, ti = br + cr, bi + ci
    er, ei = (br - cr) * (orient * math.sqrt(0.75)), (bi - ci) * (orient * math.sqrt(0.75))
    mr, mi = ar - 0.5 * tr, ai - 0.5 * ti
    return (ar + tr, ai + ti), (mr + ei, mi - er), (mr - ei, mi + er)


def dft_six(x, orient):
    out = [None] * 6
    for k1 in range(2):
        sums = []
        for n2 in range(3):
            (ar, ai), (br, bi) = x[(2 * n2) % 6], x[(3 + 2 * n2) % 6]
            sums.append((ar + br, ai + bi) if k1 == 0 else (ar - br, ai - bi))
        three = dft_three(sums, orient)
        for k2 in range(3):
            out[(3 * k1 + 4 * k2) % 6] = three[k2]
    return out


def pack(y, first, row, fold):
    for i in range(y.shape[0] // SLABS):
        block = y[SLABS * i : SLABS * i + SLABS]
        fold[pl.ds(first + i, SLABS, stride=8), :] = block[:, :128]
        tail = block[:, 128:]
        if first + i > 0:
            tail = pltpu.roll(tail, 16 * (first + i), 1)
        row = tail if row is None else row + tail
    return row


def finish_pack(row, main, rest, fold):
    main[...] = fold[...].reshape(SLABS, 8, 128).astype(BF16)
    rest[...] = row.reshape(SLABS, 1, 128)


def unpack(main, rest, fold):
    fold[...] = main[...].astype(F32).reshape(512, 128)
    row = rest[...].reshape(SLABS, 128)
    blocks = []
    for i in range(8):
        tail = pltpu.roll(row, 128 - 16 * i, 1) if i else row
        blocks.append(jnp.concatenate([fold[pl.ds(i, SLABS, stride=8), :], tail], axis=1))
    return jnp.concatenate(blocks, axis=0).astype(BF16)


def hop(a, n):
    return min(a, n - a)


def slab_order():
    offs = [(y, z, c) for y in range(4) for z in range(8) for c in range(2)][1:]
    offs.sort(key=lambda t: -(1.5 * hop(t[0], 4) + hop(t[1], 8) + 1.2 * t[2]))
    return offs


def final_order():
    tail = sorted((p for p in range(SLABS) if p not in EARLY), key=lambda p: (p * 29) % SLABS)
    return list(EARLY) + tail


def kernel(inc_hbm, trans_hbm, phase_hbm, cot_hbm, rows_hbm, cols_hbm, half_fwd_hbm, half_inv_hbm, row_tw_hbm,
           col_tw_hbm, out, field, phase, rows, cols, half_fwd, half_inv, row_tw, col_tw,
           tbuf, cur, zbuf, zcol, fold, send1, send1r, recv1, recv1r, send2, send2r, recv2, recv2r,
           recv3, recv3r, results, hbuf, outgoing,
           load, load_mat, a2a_send, a2a_recv, t_send, t_recv, r_send, r_recv):
    depth = lax.axis_index("depth")
    slab = lax.axis_index("slab")
    y0, z0, c0 = slab // 16, (slab // 2) % 8, slab % 2
    forward = depth >= 2
    adjoint = depth < 2
    which_field = lax.rem(depth, 2)
    partners = [
        lax.rem(y0 + dy, 4) * 16 + lax.rem(z0 + dz, 8) * 2 + lax.rem(c0 + dc, 2)
        for dy, dz, dc in slab_order()
    ]
    others = [lax.rem(depth + o, DEPTH) for o in range(1, DEPTH)]

    barrier = pltpu.get_barrier_semaphore()
    for p in partners:
        pl.semaphore_signal(barrier, inc=1, device_id=(depth, p), device_id_type=MESH)
    for d in others:
        pl.semaphore_signal(barrier, inc=1, device_id=(d, slab), device_id_type=MESH)

    @pl.when(adjoint)
    def _():
        pltpu.make_async_copy(cot_hbm.at[which_field], field, load.at[0]).start()

    @pl.when(forward)
    def _():
        pltpu.make_async_copy(inc_hbm.at[which_field], field, load.at[0]).start()

    loads = [
        pltpu.make_async_copy(row_tw_hbm, row_tw, load.at[1]),
        pltpu.make_async_copy(col_tw_hbm, col_tw, load.at[2]),
        pltpu.make_async_copy(phase_hbm, phase, load.at[3]),
        pltpu.make_async_copy(trans_hbm, tbuf.at[depth], load.at[4]),
    ]
    mat_loads = [
        pltpu.make_async_copy(rows_hbm, rows, load_mat.at[0]),
        pltpu.make_async_copy(cols_hbm, cols, load_mat.at[1]),
        pltpu.make_async_copy(half_fwd_hbm, half_fwd, load_mat.at[2]),
        pltpu.make_async_copy(half_inv_hbm, half_inv, load_mat.at[3]),
    ]
    loads[0].start()
    mat_loads[0].start()
    for copy in loads[1:] + mat_loads[1:]:
        copy.start()

    @pl.when(depth == 0)
    def _():
        for m in range(2):
            pltpu.make_async_copy(inc_hbm.at[m], results.at[2 + m], load.at[5 + m]).start()

    zbuf[144:, :] = jnp.zeros((112, 512), F32)
    zcol[:, 144:, :] = jnp.zeros((2, 112, 256), F32)
    hbuf[0] = jnp.zeros((2, 96, 256), F32)
    orient = jnp.where(forward, 1.0, -1.0).astype(F32)

    def t_copy(d):
        return pltpu.make_async_remote_copy(
            src_ref=trans_hbm, dst_ref=tbuf.at[depth], send_sem=t_send.at[d], recv_sem=t_recv.at[depth],
            device_id=(d, slab), device_id_type=MESH)

    def t_needed(source, target):
        return jnp.where(target < 2, source >= 1, source <= 2)

    def t_arrived(which):
        @pl.when(which != depth)
        def _():
            pltpu.make_async_copy(field, tbuf.at[which], t_recv.at[which]).wait()

    def multiply(values, which):
        f = values.astype(F32)
        t = tbuf[which].astype(F32)
        fr, fi, tr, ti = f[:ROWS], f[ROWS:], t[:ROWS], t[ROWS:] * orient
        cur[:ROWS] = (fr * tr - fi * ti).astype(BF16).astype(F32)
        cur[ROWS:] = (fr * ti + fi * tr).astype(BF16).astype(F32)

    def send_to(which, plane, p, sent, sent_rest, received, received_rest):
        pltpu.make_async_remote_copy(
            src_ref=sent.at[p], dst_ref=received.at[slab], send_sem=a2a_send.at[which, 0],
            recv_sem=a2a_recv.at[which, 0], device_id=(plane, p), device_id_type=MESH).start()
        pltpu.make_async_remote_copy(
            src_ref=sent_rest.at[p], dst_ref=received_rest.at[slab], send_sem=a2a_send.at[which, 1],
            recv_sem=a2a_recv.at[which, 1], device_id=(plane, p), device_id_type=MESH).start()

    def exchange(which, sent, sent_rest, received, received_rest):
        for p in partners:
            send_to(which, depth, p, sent, sent_rest, received, received_rest)
        received[slab] = sent[slab]
        received_rest[slab] = sent_rest[slab]

    def wait_all(sem, which, count, main, rest):
        for k, ref in enumerate((main, rest)):
            part = ref.at[pl.ds(0, count)]
            pltpu.make_async_copy(part, part, sem.at[which, k]).wait()

    def stage_a():
        for half in range(2):
            lo = 128 * half
            x = [(cur[:ROWS, BIG * a + lo : BIG * a + lo + 128], cur[ROWS:, BIG * a + lo : BIG * a + lo + 128])
                 for a in range(SMALL)]
            for j, (zr, zi) in enumerate(dft_six(x, 1.0)):
                c = row_tw[0, j : j + 1, lo : lo + 128]
                s = row_tw[1, j : j + 1, lo : lo + 128]
                zbuf[ROWS * j : ROWS * j + ROWS, lo : lo + 128] = zr * c + zi * s
                zbuf[ROWS * j : ROWS * j + ROWS, BIG + lo : BIG + lo + 128] = zi * c - zr * s
        row = pack(dot(rows[...], zbuf[...].astype(BF16), ((1,), (1,))), 0, None, fold)
        finish_pack(row, send1, send1r, fold)

    def make_filter():
        lane = lax.broadcasted_iota(jnp.int32, (SMALL, 128), 1)
        for p in range(ROWS):
            lo = 128 * (p // 2)
            for h in range(2):
                low = phase[12 * h : 12 * h + SMALL, lo : lo + 128]
                high = phase[12 * h + SMALL : 12 * h + 12, lo : lo + 128]
                if p % 2 == 0:
                    high = pltpu.roll(high, 64, 1)
                else:
                    low = pltpu.roll(low, 64, 1)
                angles = jnp.where(lane < 64, low, high)
                for g in range(2):
                    hbuf[0, h, 4 * p : 4 * p + GROUP, 128 * g : 128 * g + 128] = (
                        angles[GROUP * g : GROUP * g + GROUP])
        angles = hbuf[0]
        hbuf[0] = jnp.cos(angles)
        hbuf[1] = jnp.sin(angles) * orient

    def stage_b():
        x = unpack(recv1, recv1r, fold)[:, :144]
        c, s = col_tw[0], col_tw[1]
        cs, ss = c * (1.0 / N), s * (1.0 / N)
        halves = [dot(x[256 * h : 256 * h + 256], cols[0], ((0,), (0,))) for h in range(2)]
        for h, y in enumerate(halves):
            parts = [[], []]
            for i in range(GROUP):
                wide = [[], []]
                for g in range(2):
                    j = GROUP * g + i
                    yr, yi = y[ROWS * j : ROWS * j + ROWS, :128], y[ROWS * j : ROWS * j + ROWS, 128:]
                    wide[0].append(yr * c + yi * s)
                    wide[1].append(yi * c - yr * s)
                parts[0].append(jnp.concatenate(wide[0], axis=1))
                parts[1].append(jnp.concatenate(wide[1], axis=1))
            halves[h] = jnp.concatenate(parts[0] + parts[1], axis=0).astype(BF16)
        halves = [dot(half_fwd[...], x) for x in halves]
        for h, x in enumerate(halves):
            xr, xi, hr, hi = x[:96], x[96:], hbuf[0, h], hbuf[1, h]
            halves[h] = jnp.concatenate([xr * hr - xi * hi, xi * hr + xr * hi], axis=0).astype(BF16)
        halves = [dot(half_inv[...], x) for x in halves]
        for h, x in enumerate(halves):
            for i in range(GROUP):
                for g in range(2):
                    j = GROUP * g + i
                    xr = x[ROWS * i : ROWS * i + ROWS, 128 * g : 128 * g + 128]
                    xi = x[72 + ROWS * i : 72 + ROWS * i + ROWS, 128 * g : 128 * g + 128]
                    zcol[h, ROWS * j : ROWS * j + ROWS, :128] = xr * cs - xi * ss
                    zcol[h, ROWS * j : ROWS * j + ROWS, 128:] = xi * cs + xr * ss
        halves = [dot(cols[1], zcol[h].astype(BF16), ((1,), (1,))) for h in range(2)]
        row = None
        for h, y in enumerate(halves):
            row = pack(y, 4 * h, row, fold)
        finish_pack(row, send2, send2r, fold)

    def store(target, index):
        def put(a, lo, vr, vi):
            both = jnp.concatenate([vr, vi], axis=0)
            target[index, :, BIG * a + lo : BIG * a + lo + 128] = both.astype(BF16)

        return put

    def add_product(m):
        def put(a, lo, vr, vi):
            at = pl.ds(BIG * a + lo, 128)
            u = results[2 + m, :, at].astype(F32)
            ur, ui = u[:ROWS], u[ROWS:]
            pr, pi = vr.astype(BF16).astype(F32), vi.astype(BF16).astype(F32)
            gr, gi = ur * pr + ui * pi, ur * pi - ui * pr
            if m > 0:
                gr, gi = out[:ROWS, at] + gr, out[ROWS:, at] + gi
            out[:ROWS, at] = gr
            out[ROWS:, at] = gi

        return put

    def stage_c(main, rest, put):
        zbuf_c = dot(unpack(main, rest, fold)[:, :144], rows[...], ((0,), (0,)))
        for half in range(2):
            lo = 128 * half
            x = []
            for j in range(SMALL):
                c = row_tw[0, j : j + 1, lo : lo + 128] * (1.0 / N)
                s = row_tw[1, j : j + 1, lo : lo + 128] * (1.0 / N)
                zr = zbuf_c[ROWS * j : ROWS * j + ROWS, lo : lo + 128]
                zi = zbuf_c[ROWS * j : ROWS * j + ROWS, BIG + lo : BIG + lo + 128]
                x.append((zr * c - zi * s, zi * c + zr * s))
            for a, (vr, vi) in enumerate(dft_six(x, -1.0)):
                put(a, lo, vr, vi)

    def r_copy(turn, target):
        return pltpu.make_async_remote_copy(
            src_ref=outgoing.at[turn], dst_ref=results.at[depth], send_sem=r_send.at[turn],
            recv_sem=r_recv.at[depth], device_id=(target, slab), device_id_type=MESH)

    def target_of(turn):
        return jnp.where(forward, turn + 1, DEPTH - 1 - turn)

    pltpu.make_async_copy(inc_hbm.at[0], field, load.at[0]).wait()
    loads[0].wait()
    mat_loads[0].wait()

    @pl.when(adjoint)
    def _():
        cur[...] = field[...].astype(F32)
        stage_a()

    loads[3].wait()
    loads[2].wait()
    make_filter()
    pl.semaphore_wait(barrier, len(partners) + len(others))

    for d in others:
        @pl.when(t_needed(depth, d))
        def _(d=d):
            t_copy(d).start()

    @pl.when(forward)
    def _():
        t_arrived(0)
        multiply(field[...], 0)
        stage_a()

    for copy in loads[1:2] + mat_loads[1:]:
        copy.wait()

    first = send1, send1r, recv1, recv1r
    second = send2, send2r, recv2, recv2r
    last = DEPTH - 1
    most = SLABS - 1

    @pl.loop(0, DEPTH)
    def _(turn):
        @pl.when(adjoint | (turn < last))
        def _():
            exchange(0, *first)
            wait_all(a2a_recv, 0, most, recv1, recv1r)

            @pl.when(turn > 0)
            def _():
                wait_all(a2a_send, 1, most, send2, send2r)

            stage_b()
            direct = (depth == 1) & (turn == last)

            @pl.when(direct)
            def _():
                pltpu.make_async_copy(field, results.at[0], r_recv.at[0]).wait()
                for p in final_order():
                    send_to(2, 0, p, send2, send2r, recv3, recv3r)
                wait_all(a2a_send, 0, most, send1, send1r)

            @pl.when(jnp.logical_not(direct))
            def _():
                @pl.when(turn < last)
                def _():
                    exchange(1, *second)

                @pl.when(turn == last)
                def _():
                    for p in final_order():
                        @pl.when(p != slab)
                        def _(p=p):
                            send_to(1, 0, p, *second)
                    recv2[slab] = send2[slab]
                    recv2r[slab] = send2r[slab]

                target = target_of(turn)
                wait_all(a2a_recv, 1, most, recv2, recv2r)
                wait_all(a2a_send, 0, most, send1, send1r)

                @pl.when(turn < last)
                def _():
                    stage_c(recv2, recv2r, store(outgoing, turn))

                @pl.when(target != depth)
                def _():
                    r_copy(turn, target).start()

                @pl.when((target == depth) & (turn < last))
                def _():
                    results[depth] = outgoing[turn]

                @pl.when(jnp.where(forward, turn < last - 1, turn < last))
                def _():
                    t_arrived(target)
                    multiply(outgoing[turn], target)
                    stage_a()

    @pl.when(depth == 0)
    def _():
        for m in range(2):
            pltpu.make_async_copy(inc_hbm.at[m], results.at[2 + m], load.at[5 + m]).wait()
        stage_c(recv2, recv2r, add_product(0))
        wait_all(a2a_recv, 2, SLABS, recv3, recv3r)
        stage_c(recv3, recv3r, add_product(1))

    for slot, needed in ((0, depth >= 2), (1, depth >= 2), (2, (depth == 1) | (depth == 3)), (3, (depth == 1) | (depth == 2))):
        @pl.when(needed)
        def _(slot=slot):
            pltpu.make_async_copy(field, results.at[slot], r_recv.at[slot]).wait()

    @pl.when(depth > 0)
    def _():
        gr = jnp.zeros((ROWS, N), F32)
        gi = jnp.zeros((ROWS, N), F32)
        for m in range(2):
            u = results[2 + m].astype(F32)
            p = results[m].astype(F32)
            ur, ui, pr, pi = u[:ROWS], u[ROWS:], p[:ROWS], p[ROWS:]
            gr = gr + (ur * pr + ui * pi)
            gi = gi + (ur * pi - ui * pr)
        out[:ROWS] = gr
        out[ROWS:] = gi

    for d in others:
        @pl.when(t_needed(depth, d))
        def _(d=d):
            t_copy(d).wait_send()

    for turn in range(last):
        target = target_of(turn)

        @pl.when(target != depth)
        def _(turn=turn, target=target):
            r_copy(turn, target).wait_send()

    @pl.when(depth == 1)
    def _():
        wait_all(a2a_send, 2, SLABS, send2, send2r)

    @pl.when(depth != 1)
    def _():
        wait_all(a2a_send, 1, most, send2, send2r)


def on_device(incident, transmission, prop_phase, cotangent):
    rows, cols, half_fwd, half_inv, row_tw, col_tw = (jnp.asarray(t) for t in make_tables())
    inc = incident.reshape(2, 2 * ROWS, N)
    trans = transmission.reshape(2 * ROWS, N)
    cot = cotangent.reshape(2, 2 * ROWS, N)
    hbm = pl.BlockSpec(memory_space=pltpu.HBM)
    field = (2 * ROWS, N)
    main = pltpu.VMEM((SLABS, 8, 128), BF16)
    rest = pltpu.VMEM((SLABS, 1, 128), F32)
    dma = pltpu.SemaphoreType.DMA
    grads = pl.pallas_call(
        kernel,
        out_shape=jax.ShapeDtypeStruct(field, F32),
        in_specs=[hbm] * 10,
        out_specs=pl.BlockSpec(memory_space=pltpu.VMEM),
        scratch_shapes=[
            pltpu.VMEM(field, BF16),
            pltpu.VMEM((ROWS, N), F32),
            pltpu.VMEM(rows.shape, BF16),
            pltpu.VMEM(cols.shape, BF16),
            pltpu.VMEM(half_fwd.shape, BF16),
            pltpu.VMEM(half_inv.shape, BF16),
            pltpu.VMEM(row_tw.shape, F32),
            pltpu.VMEM(col_tw.shape, F32),
            pltpu.VMEM((DEPTH,) + field, BF16),
            pltpu.VMEM(field, F32),
            pltpu.VMEM((256, 512), F32),
            pltpu.VMEM((2, 256, 256), F32),
            pltpu.VMEM((512, 128), F32),
            main, rest, main, rest, main, rest, main, rest, main, rest,
            pltpu.VMEM((DEPTH,) + field, BF16),
            pltpu.VMEM((2, 2, 96, 256), F32),
            pltpu.VMEM((DEPTH,) + field, BF16),
            dma((7,)), dma((4,)), dma((3, 2)), dma((3, 2)),
            dma((DEPTH,)), dma((DEPTH,)), dma((DEPTH,)), dma((DEPTH,)),
        ],
        compiler_params=pltpu.CompilerParams(
            collective_id=0, has_side_effects=True, vmem_limit_bytes=62 * 2**20),
        name="chains",
    )(inc, trans, prop_phase.T, cot, rows, cols, half_fwd, half_inv, row_tw, col_tw)
    return grads.reshape(1, 2, ROWS, N)


def solution(mesh):
    in_specs = (
        P(None, None, "slab", None),
        P("depth", None, "slab", None),
        P(None, "slab"),
        P(None, None, "slab", None),
    )
    out_specs = P("depth", None, "slab", None)
    return jax.shard_map(
        on_device, mesh=mesh, in_specs=in_specs, out_specs=out_specs, check_vma=False
    )
```

```python
import functools
import math

import jax
import jax.numpy as jnp
import numpy as np
from jax import lax
from jax.experimental import pallas as pl
from jax.experimental.pallas import tpu as pltpu
from jax.sharding import PartitionSpec as P

N = 1536
SLABS = 64
ROWS = N // SLABS
BIG = 256
SMALL = N // BIG
KEEP = BIG // SLABS
DEPTH = 4
GROUP = SMALL // 2
EARLY = (0, 1, 8, 2, 9)
MESH = pl.DeviceIdType.MESH
F32 = jnp.float32
BF16 = jnp.bfloat16


def angle(x, period):
    turn = 2.0 * math.pi * (x % period) / period
    return np.cos(turn), np.sin(turn)


def block_matrix(re_re, re_im, im_re, im_im):
    return np.block([[re_re, re_im], [im_re, im_im]])


@functools.lru_cache(None)
def make_tables():
    bf = lambda a: np.asarray(a, np.float32).astype(jnp.bfloat16)
    freq = np.arange(BIG)
    samp = np.arange(BIG)
    cos, sin = angle(freq[:, None] * samp[None, :], BIG)
    cos = cos.reshape(SLABS, 2, 2, BIG).transpose(1, 2, 0, 3)
    sin = sin.reshape(SLABS, 2, 2, BIG).transpose(1, 2, 0, 3)
    full = np.zeros((2, 2, 2, SLABS, 2, BIG))
    full[:, 0, :, :, 0], full[:, 0, :, :, 1] = cos, sin
    full[:, 1, :, :, 0], full[:, 1, :, :, 1] = -sin, cos
    rows = full.reshape(512, 512)
    m64 = np.arange(SLABS)
    cos, sin = angle(m64[:, None] * m64[None, :], SLABS)
    full = np.zeros((2, 2, SLABS, 2, 2, SLABS))
    back = np.zeros((2, 2, SLABS, 2, 2, SLABS))
    for k in range(2):
        full[0, k, :, 0, k], full[1, k, :, 0, k] = cos, sin
        full[0, k, :, 1, k], full[1, k, :, 1, k] = -sin, cos
        back[0, k, :, 0, k], back[0, k, :, 1, k] = cos, -sin
        back[1, k, :, 0, k], back[1, k, :, 1, k] = sin, cos
    cols = np.stack([full.reshape(256, 256), back.reshape(256, 256)])
    half_fwd = np.zeros((2, 96, 2, 72))
    half_inv = np.zeros((2, 72, 2, 96))
    rho = np.arange(ROWS)
    cos, sin = angle(rho[:, None] * rho[None, :], ROWS)
    for j in range(GROUP):
        a = 24 * j + rho[None, :]
        b = 4 * rho[:, None] + j
        half_fwd[0, b, 0, a], half_fwd[0, b, 1, a] = cos, sin
        half_fwd[1, b, 0, a], half_fwd[1, b, 1, a] = -sin, cos
        half_inv[0, a, 0, b], half_inv[0, a, 1, b] = cos, -sin
        half_inv[1, a, 0, b], half_inv[1, a, 1, b] = sin, cos
    half_fwd = half_fwd.reshape(192, 144)
    half_inv = half_inv.reshape(144, 192)
    cos, sin = angle(np.arange(SMALL)[:, None] * samp[None, :], N)
    row_tw = np.zeros((2, 8, BIG))
    row_tw[0, :SMALL], row_tw[1, :SMALL] = cos, sin
    cos, sin = angle(rho[:, None] * m64[None, :], N)
    col_tw = np.stack([np.tile(cos, (1, 2)), np.tile(sin, (1, 2))])
    f32 = lambda a: np.asarray(a, np.float32)
    return bf(rows), bf(cols), bf(half_fwd), bf(half_inv), f32(row_tw), f32(col_tw)


def dot(a, b, dims=((1,), (0,))):
    return lax.dot_general(a, b, (dims, ((), ())), preferred_element_type=F32)


def dft_three(x, orient):
    (ar, ai), (br, bi), (cr, ci) = x
    tr, ti = br + cr, bi + ci
    er, ei = (br - cr) * (orient * math.sqrt(0.75)), (bi - ci) * (orient * math.sqrt(0.75))
    mr, mi = ar - 0.5 * tr, ai - 0.5 * ti
    return (ar + tr, ai + ti), (mr + ei, mi - er), (mr - ei, mi + er)


def dft_six(x, orient):
    out = [None] * 6
    for k1 in range(2):
        sums = []
        for n2 in range(3):
            (ar, ai), (br, bi) = x[(2 * n2) % 6], x[(3 + 2 * n2) % 6]
            sums.append((ar + br, ai + bi) if k1 == 0 else (ar - br, ai - bi))
        three = dft_three(sums, orient)
        for k2 in range(3):
            out[(3 * k1 + 4 * k2) % 6] = three[k2]
    return out


def pack(y, first, row, fold):
    for i in range(y.shape[0] // SLABS):
        block = y[SLABS * i : SLABS * i + SLABS]
        fold[pl.ds(first + i, SLABS, stride=8), :] = block[:, :128]
        tail = block[:, 128:]
        if first + i > 0:
            tail = pltpu.roll(tail, 16 * (first + i), 1)
        row = tail if row is None else row + tail
    return row


def finish_pack(row, main, rest, fold):
    main[...] = fold[...].reshape(SLABS, 8, 128).astype(BF16)
    rest[...] = row.reshape(SLABS, 1, 128)


def unpack(main, rest, fold):
    fold[...] = main[...].astype(F32).reshape(512, 128)
    row = rest[...].reshape(SLABS, 128)
    blocks = []
    for i in range(8):
        tail = pltpu.roll(row, 128 - 16 * i, 1) if i else row
        blocks.append(jnp.concatenate([fold[pl.ds(i, SLABS, stride=8), :], tail], axis=1))
    return jnp.concatenate(blocks, axis=0).astype(BF16)


def hop(a, n):
    return min(a, n - a)


def slab_order():
    offs = [(y, z, c) for y in range(4) for z in range(8) for c in range(2)][1:]
    offs.sort(key=lambda t: -(1.5 * hop(t[0], 4) + hop(t[1], 8) + 1.2 * t[2]))
    return offs


def final_order(core):
    early = [2 * q + c for q in EARLY for c in (1, 0)]
    late = sorted((q for q in range(SLABS // 2) if q not in EARLY), key=lambda q: (q * 13) % 32)
    return early + [2 * q + 1 - core for q in late] + [2 * q + core for q in late]


def kernel(inc_hbm, trans_hbm, phase_hbm, cot_hbm, rows_hbm, cols_hbm, half_fwd_hbm, half_inv_hbm, row_tw_hbm,
           col_tw_hbm, out, field, phase, rows, cols, half_fwd, half_inv, row_tw, col_tw,
           tbuf, cur, zbuf, zcol, fold, send1, send1r, recv1, recv1r, send2, send2r, recv2, recv2r,
           recv3, recv3r, results, hbuf, outgoing,
           load, load_mat, a2a_send, a2a_recv, t_send, t_recv, r_send, r_recv):
    depth = lax.axis_index("depth")
    slab = lax.axis_index("slab")
    y0, z0, c0 = slab // 16, (slab // 2) % 8, slab % 2
    forward = depth >= 2
    adjoint = depth < 2
    which_field = lax.rem(depth, 2)
    partners = [
        lax.rem(y0 + dy, 4) * 16 + lax.rem(z0 + dz, 8) * 2 + lax.rem(c0 + dc, 2)
        for dy, dz, dc in slab_order()
    ]
    others = [lax.rem(depth + o, DEPTH) for o in range(1, DEPTH)]

    barrier = pltpu.get_barrier_semaphore()
    for p in partners:
        pl.semaphore_signal(barrier, inc=1, device_id=(depth, p), device_id_type=MESH)
    for d in others:
        pl.semaphore_signal(barrier, inc=1, device_id=(d, slab), device_id_type=MESH)

    @pl.when(adjoint)
    def _():
        pltpu.make_async_copy(cot_hbm.at[which_field], field, load.at[0]).start()

    @pl.when(forward)
    def _():
        pltpu.make_async_copy(inc_hbm.at[which_field], field, load.at[0]).start()

    loads = [
        pltpu.make_async_copy(row_tw_hbm, row_tw, load.at[1]),
        pltpu.make_async_copy(col_tw_hbm, col_tw, load.at[2]),
        pltpu.make_async_copy(phase_hbm, phase, load.at[3]),
        pltpu.make_async_copy(trans_hbm, tbuf.at[depth], load.at[4]),
    ]
    mat_loads = [
        pltpu.make_async_copy(rows_hbm, rows, load_mat.at[0]),
        pltpu.make_async_copy(cols_hbm, cols, load_mat.at[1]),
        pltpu.make_async_copy(half_fwd_hbm, half_fwd, load_mat.at[2]),
        pltpu.make_async_copy(half_inv_hbm, half_inv, load_mat.at[3]),
    ]
    loads[0].start()
    mat_loads[0].start()
    for copy in loads[1:] + mat_loads[1:]:
        copy.start()

    @pl.when(depth == 0)
    def _():
        for m in range(2):
            pltpu.make_async_copy(inc_hbm.at[m], results.at[2 + m], load.at[5 + m]).start()

    zbuf[144:, :] = jnp.zeros((112, 512), F32)
    zcol[:, 144:, :] = jnp.zeros((2, 112, 256), F32)
    hbuf[0] = jnp.zeros((2, 96, 256), F32)
    orient = jnp.where(forward, 1.0, -1.0).astype(F32)

    def t_copy(d):
        return pltpu.make_async_remote_copy(
            src_ref=trans_hbm, dst_ref=tbuf.at[depth], send_sem=t_send.at[d], recv_sem=t_recv.at[depth],
            device_id=(d, slab), device_id_type=MESH)

    def t_needed(source, target):
        return jnp.where(target < 2, source >= 1, source <= 2)

    def t_arrived(which):
        @pl.when(which != depth)
        def _():
            pltpu.make_async_copy(field, tbuf.at[which], t_recv.at[which]).wait()

    def multiply(values, which):
        f = values.astype(F32)
        t = tbuf[which].astype(F32)
        fr, fi, tr, ti = f[:ROWS], f[ROWS:], t[:ROWS], t[ROWS:] * orient
        cur[:ROWS] = (fr * tr - fi * ti).astype(BF16).astype(F32)
        cur[ROWS:] = (fr * ti + fi * tr).astype(BF16).astype(F32)

    def send_to(which, plane, p, sent, sent_rest, received, received_rest):
        pltpu.make_async_remote_copy(
            src_ref=sent.at[p], dst_ref=received.at[slab], send_sem=a2a_send.at[which, 0],
            recv_sem=a2a_recv.at[which, 0], device_id=(plane, p), device_id_type=MESH).start()
        pltpu.make_async_remote_copy(
            src_ref=sent_rest.at[p], dst_ref=received_rest.at[slab], send_sem=a2a_send.at[which, 1],
            recv_sem=a2a_recv.at[which, 1], device_id=(plane, p), device_id_type=MESH).start()

    def exchange(which, sent, sent_rest, received, received_rest):
        for p in partners:
            send_to(which, depth, p, sent, sent_rest, received, received_rest)
        received[slab] = sent[slab]
        received_rest[slab] = sent_rest[slab]

    def wait_all(sem, which, count, main, rest):
        for k, ref in enumerate((main, rest)):
            part = ref.at[pl.ds(0, count)]
            pltpu.make_async_copy(part, part, sem.at[which, k]).wait()

    def stage_a():
        for half in range(2):
            lo = 128 * half
            x = [(cur[:ROWS, BIG * a + lo : BIG * a + lo + 128], cur[ROWS:, BIG * a + lo : BIG * a + lo + 128])
                 for a in range(SMALL)]
            for j, (zr, zi) in enumerate(dft_six(x, 1.0)):
                c = row_tw[0, j : j + 1, lo : lo + 128]
                s = row_tw[1, j : j + 1, lo : lo + 128]
                zbuf[ROWS * j : ROWS * j + ROWS, lo : lo + 128] = zr * c + zi * s
                zbuf[ROWS * j : ROWS * j + ROWS, BIG + lo : BIG + lo + 128] = zi * c - zr * s
        row = pack(dot(rows[...], zbuf[...].astype(BF16), ((1,), (1,))), 0, None, fold)
        finish_pack(row, send1, send1r, fold)

    def make_filter():
        lane = lax.broadcasted_iota(jnp.int32, (SMALL, 128), 1)
        for p in range(ROWS):
            lo = 128 * (p // 2)
            for h in range(2):
                low = phase[12 * h : 12 * h + SMALL, lo : lo + 128]
                high = phase[12 * h + SMALL : 12 * h + 12, lo : lo + 128]
                if p % 2 == 0:
                    high = pltpu.roll(high, 64, 1)
                else:
                    low = pltpu.roll(low, 64, 1)
                angles = jnp.where(lane < 64, low, high)
                for g in range(2):
                    hbuf[0, h, 4 * p : 4 * p + GROUP, 128 * g : 128 * g + 128] = (
                        angles[GROUP * g : GROUP * g + GROUP])
        angles = hbuf[0]
        hbuf[0] = jnp.cos(angles)
        hbuf[1] = jnp.sin(angles) * orient

    def stage_b():
        x = unpack(recv1, recv1r, fold)[:, :144]
        c, s = col_tw[0], col_tw[1]
        cs, ss = c * (1.0 / N), s * (1.0 / N)
        halves = [dot(x[256 * h : 256 * h + 256], cols[0], ((0,), (0,))) for h in range(2)]
        for h, y in enumerate(halves):
            parts = [[], []]
            for i in range(GROUP):
                wide = [[], []]
                for g in range(2):
                    j = GROUP * g + i
                    yr, yi = y[ROWS * j : ROWS * j + ROWS, :128], y[ROWS * j : ROWS * j + ROWS, 128:]
                    wide[0].append(yr * c + yi * s)
                    wide[1].append(yi * c - yr * s)
                parts[0].append(jnp.concatenate(wide[0], axis=1))
                parts[1].append(jnp.concatenate(wide[1], axis=1))
            halves[h] = jnp.concatenate(parts[0] + parts[1], axis=0).astype(BF16)
        halves = [dot(half_fwd[...], x) for x in halves]
        for h, x in enumerate(halves):
            xr, xi, hr, hi = x[:96], x[96:], hbuf[0, h], hbuf[1, h]
            halves[h] = jnp.concatenate([xr * hr - xi * hi, xi * hr + xr * hi], axis=0).astype(BF16)
        halves = [dot(half_inv[...], x) for x in halves]
        for h, x in enumerate(halves):
            for i in range(GROUP):
                for g in range(2):
                    j = GROUP * g + i
                    xr = x[ROWS * i : ROWS * i + ROWS, 128 * g : 128 * g + 128]
                    xi = x[72 + ROWS * i : 72 + ROWS * i + ROWS, 128 * g : 128 * g + 128]
                    zcol[h, ROWS * j : ROWS * j + ROWS, :128] = xr * cs - xi * ss
                    zcol[h, ROWS * j : ROWS * j + ROWS, 128:] = xi * cs + xr * ss
        halves = [dot(cols[1], zcol[h].astype(BF16), ((1,), (1,))) for h in range(2)]
        row = None
        for h, y in enumerate(halves):
            row = pack(y, 4 * h, row, fold)
        finish_pack(row, send2, send2r, fold)

    def store(target, index):
        def put(a, lo, vr, vi):
            both = jnp.concatenate([vr, vi], axis=0)
            target[index, :, BIG * a + lo : BIG * a + lo + 128] = both.astype(BF16)

        return put

    def add_product(m):
        def put(a, lo, vr, vi):
            at = pl.ds(BIG * a + lo, 128)
            u = results[2 + m, :, at].astype(F32)
            ur, ui = u[:ROWS], u[ROWS:]
            pr, pi = vr.astype(BF16).astype(F32), vi.astype(BF16).astype(F32)
            gr, gi = ur * pr + ui * pi, ur * pi - ui * pr
            if m > 0:
                gr, gi = out[:ROWS, at] + gr, out[ROWS:, at] + gi
            out[:ROWS, at] = gr
            out[ROWS:, at] = gi

        return put

    def stage_c(main, rest, put):
        zbuf_c = dot(unpack(main, rest, fold)[:, :144], rows[...], ((0,), (0,)))
        for half in range(2):
            lo = 128 * half
            x = []
            for j in range(SMALL):
                c = row_tw[0, j : j + 1, lo : lo + 128] * (1.0 / N)
                s = row_tw[1, j : j + 1, lo : lo + 128] * (1.0 / N)
                zr = zbuf_c[ROWS * j : ROWS * j + ROWS, lo : lo + 128]
                zi = zbuf_c[ROWS * j : ROWS * j + ROWS, BIG + lo : BIG + lo + 128]
                x.append((zr * c - zi * s, zi * c + zr * s))
            for a, (vr, vi) in enumerate(dft_six(x, -1.0)):
                put(a, lo, vr, vi)

    def r_copy(turn, target):
        return pltpu.make_async_remote_copy(
            src_ref=outgoing.at[turn], dst_ref=results.at[depth], send_sem=r_send.at[turn],
            recv_sem=r_recv.at[depth], device_id=(target, slab), device_id_type=MESH)

    def target_of(turn):
        return jnp.where(forward, turn + 1, DEPTH - 1 - turn)

    pltpu.make_async_copy(inc_hbm.at[0], field, load.at[0]).wait()
    loads[0].wait()
    mat_loads[0].wait()

    @pl.when(adjoint)
    def _():
        cur[...] = field[...].astype(F32)
        stage_a()

    loads[3].wait()
    loads[2].wait()
    make_filter()
    pl.semaphore_wait(barrier, len(partners) + len(others))

    for d in others:
        @pl.when(t_needed(depth, d))
        def _(d=d):
            t_copy(d).start()

    @pl.when(forward)
    def _():
        t_arrived(0)
        multiply(field[...], 0)
        stage_a()

    for copy in loads[1:2] + mat_loads[1:]:
        copy.wait()

    first = send1, send1r, recv1, recv1r
    second = send2, send2r, recv2, recv2r
    last = DEPTH - 1
    most = SLABS - 1

    @pl.loop(0, DEPTH)
    def _(turn):
        @pl.when(adjoint | (turn < last))
        def _():
            exchange(0, *first)
            wait_all(a2a_recv, 0, most, recv1, recv1r)

            @pl.when(turn > 0)
            def _():
                wait_all(a2a_send, 1, most, send2, send2r)

            stage_b()
            direct = (depth == 1) & (turn == last)

            @pl.when(direct)
            def _():
                pltpu.make_async_copy(field, results.at[0], r_recv.at[0]).wait()
                for p in final_order(c0):
                    send_to(2, 0, p, send2, send2r, recv3, recv3r)
                wait_all(a2a_send, 0, most, send1, send1r)

            @pl.when(jnp.logical_not(direct))
            def _():
                @pl.when(turn < last)
                def _():
                    exchange(1, *second)

                @pl.when(turn == last)
                def _():
                    for p in final_order(c0):
                        @pl.when(p != slab)
                        def _(p=p):
                            send_to(1, 0, p, *second)
                    recv2[slab] = send2[slab]
                    recv2r[slab] = send2r[slab]

                target = target_of(turn)
                wait_all(a2a_recv, 1, most, recv2, recv2r)
                wait_all(a2a_send, 0, most, send1, send1r)

                @pl.when(turn < last)
                def _():
                    stage_c(recv2, recv2r, store(outgoing, turn))

                @pl.when(target != depth)
                def _():
                    r_copy(turn, target).start()

                @pl.when((target == depth) & (turn < last))
                def _():
                    results[depth] = outgoing[turn]

                @pl.when(jnp.where(forward, turn < last - 1, turn < last))
                def _():
                    t_arrived(target)
                    multiply(outgoing[turn], target)
                    stage_a()

    @pl.when(depth == 0)
    def _():
        for m in range(2):
            pltpu.make_async_copy(inc_hbm.at[m], results.at[2 + m], load.at[5 + m]).wait()
        stage_c(recv2, recv2r, add_product(0))
        wait_all(a2a_recv, 2, SLABS, recv3, recv3r)
        stage_c(recv3, recv3r, add_product(1))

    for slot, needed in ((0, depth >= 2), (1, depth >= 2), (2, (depth == 1) | (depth == 3)), (3, (depth == 1) | (depth == 2))):
        @pl.when(needed)
        def _(slot=slot):
            pltpu.make_async_copy(field, results.at[slot], r_recv.at[slot]).wait()

    @pl.when(depth > 0)
    def _():
        gr = jnp.zeros((ROWS, N), F32)
        gi = jnp.zeros((ROWS, N), F32)
        for m in range(2):
            u = results[2 + m].astype(F32)
            p = results[m].astype(F32)
            ur, ui, pr, pi = u[:ROWS], u[ROWS:], p[:ROWS], p[ROWS:]
            gr = gr + (ur * pr + ui * pi)
            gi = gi + (ur * pi - ui * pr)
        out[:ROWS] = gr
        out[ROWS:] = gi

    for d in others:
        @pl.when(t_needed(depth, d))
        def _(d=d):
            t_copy(d).wait_send()

    for turn in range(last):
        target = target_of(turn)

        @pl.when(target != depth)
        def _(turn=turn, target=target):
            r_copy(turn, target).wait_send()

    @pl.when(depth == 1)
    def _():
        wait_all(a2a_send, 2, SLABS, send2, send2r)

    @pl.when(depth != 1)
    def _():
        wait_all(a2a_send, 1, most, send2, send2r)


def on_device(incident, transmission, prop_phase, cotangent):
    rows, cols, half_fwd, half_inv, row_tw, col_tw = (jnp.asarray(t) for t in make_tables())
    inc = incident.reshape(2, 2 * ROWS, N)
    trans = transmission.reshape(2 * ROWS, N)
    cot = cotangent.reshape(2, 2 * ROWS, N)
    hbm = pl.BlockSpec(memory_space=pltpu.HBM)
    field = (2 * ROWS, N)
    main = pltpu.VMEM((SLABS, 8, 128), BF16)
    rest = pltpu.VMEM((SLABS, 1, 128), F32)
    dma = pltpu.SemaphoreType.DMA
    grads = pl.pallas_call(
        kernel,
        out_shape=jax.ShapeDtypeStruct(field, F32),
        in_specs=[hbm] * 10,
        out_specs=pl.BlockSpec(memory_space=pltpu.VMEM),
        scratch_shapes=[
            pltpu.VMEM(field, BF16),
            pltpu.VMEM((ROWS, N), F32),
            pltpu.VMEM(rows.shape, BF16),
            pltpu.VMEM(cols.shape, BF16),
            pltpu.VMEM(half_fwd.shape, BF16),
            pltpu.VMEM(half_inv.shape, BF16),
            pltpu.VMEM(row_tw.shape, F32),
            pltpu.VMEM(col_tw.shape, F32),
            pltpu.VMEM((DEPTH,) + field, BF16),
            pltpu.VMEM(field, F32),
            pltpu.VMEM((256, 512), F32),
            pltpu.VMEM((2, 256, 256), F32),
            pltpu.VMEM((512, 128), F32),
            main, rest, main, rest, main, rest, main, rest, main, rest,
            pltpu.VMEM((DEPTH,) + field, BF16),
            pltpu.VMEM((2, 2, 96, 256), F32),
            pltpu.VMEM((DEPTH,) + field, BF16),
            dma((7,)), dma((4,)), dma((3, 2)), dma((3, 2)),
            dma((DEPTH,)), dma((DEPTH,)), dma((DEPTH,)), dma((DEPTH,)),
        ],
        compiler_params=pltpu.CompilerParams(
            collective_id=0, has_side_effects=True, vmem_limit_bytes=62 * 2**20),
        name="chains",
    )(inc, trans, prop_phase.T, cot, rows, cols, half_fwd, half_inv, row_tw, col_tw)
    return grads.reshape(1, 2, ROWS, N)


def solution(mesh):
    in_specs = (
        P(None, None, "slab", None),
        P("depth", None, "slab", None),
        P(None, "slab"),
        P(None, None, "slab", None),
    )
    out_specs = P("depth", None, "slab", None)
    return jax.shard_map(
        on_device, mesh=mesh, in_specs=in_specs, out_specs=out_specs, check_vma=False
    )
```
